32 devices in a mesh: dp: 4 (over x, core), expert: 8 (over z, y).
Axes of the slice: x: 2, y: 2, z: 4, core: 2. Of those that a mesh axis runs over, the one named last changes fastest.
Arguments:
- tokens: bfloat16 [4096, 3072], P(('dp', 'expert')), may hold values from -6 to 6
- routes: int32 [4096, 2], P(('dp', 'expert')), may hold values from 0 to 7, as said below
- router_gates: int32 [4096, 2], P(('dp', 'expert')), may hold values from 1024 to 32767
- hidden_cotangent: bfloat16 [4096, 2, 768], P(('dp', 'expert')), may hold values from -6 to 6
- weights: bfloat16 [2, 8, 768, 3072], P(None, None, 'expert', 'dp'), may hold values from -0.109375 to 0.109375
- first_moment: bfloat16 [2, 8, 768, 3072], P(None, None, 'expert', 'dp'), may hold values from -6 to 6
- second_moment: bfloat16 [2, 8, 768, 3072], P(None, None, 'expert', 'dp'), may hold values from 0.5 to 4
Outputs:
- token_grads: bfloat16 [4096, 3072], P(('dp', 'expert'))
- new_weights: bfloat16 [2, 8, 768, 3072], P(None, 'expert', None, 'dp')
- new_first: bfloat16 [2, 8, 768, 3072], P(None, 'expert', None, 'dp')
- new_second: bfloat16 [2, 8, 768, 3072], P(None, 'expert', None, 'dp')
The draws below stay inside these ranges and needn't reach their ends.
Inputs may be any that keep to these rules, and one draw needn't show every extreme that they name: `routes`: each row names 2 different experts; the rows of one device name any one expert at most 48 times.
All inputs are finite; a program needn't handle non-finite values.
Results may differ from the reference program's by a relative error of at most 0.0075.
Values may be sent and summed in bfloat16 or wider, within the bound.
No kernel may reach another device: no remote copies, remote signals or barrier semaphores. Data moves between devices by JAX's collectives and lax.ppermute only.
A program may use at most 128 MiB of HBM per device.

```python
import math
import jax
import jax.numpy as jnp
from jax import lax

D = 3072
H = 768
TOP = 2
TOK = 128
E = 8
CAP = 48
TOKENS = 4096
N_DP = 4
N_EXPERT = 8


def draw_routes(key, part):
    key = jax.random.fold_in(key, 11)
    blocks = TOKENS // TOK
    hot_key, order_key, place_key, shift_key, other_key = jax.random.split(key, 5)
    hot_expert = jax.random.randint(hot_key, (), 0, E)
    orders = jax.vmap(lambda item: jax.random.permutation(item, TOK))(jax.random.split(order_key, blocks))
    is_hot = orders < CAP
    hot_place = jax.random.randint(place_key, (blocks, TOK), 0, TOP)
    needed = jnp.where(is_hot, TOP - 1, TOP)
    starts = jnp.cumsum(needed, axis=1) - needed
    shifts = jax.random.randint(shift_key, (blocks, 1), 0, E - 1)
    others = jax.vmap(lambda item: jax.random.permutation(item, E - 1))(jax.random.split(other_key, blocks))
    others = others + (others >= hot_expert).astype(jnp.int32)
    columns = []
    for column in range(TOP):
        offset = jnp.where(is_hot & (column > hot_place), column - 1, column)
        counter = (starts + offset + shifts) % (E - 1)
        picked = jnp.take_along_axis(others, counter, axis=1)
        columns.append(jnp.where(is_hot & (column == hot_place), hot_expert, picked))
    return jnp.stack(columns, axis=-1).reshape(TOKENS, TOP).astype(jnp.int32)


def set_ends(drawn, key, low, top_value):
    spot = [jax.random.randint(jax.random.fold_in(key, axis), (), 0, length) for axis, length in enumerate(drawn.shape)]
    main_axis = drawn.shape.index(max(drawn.shape))
    beside = spot[:main_axis] + [(spot[main_axis] + 1) % drawn.shape[main_axis]] + spot[main_axis + 1:]
    return drawn.at[tuple(spot)].set(low).at[tuple(beside)].set(top_value)


def level_of(rng, extent, pieces, low, largest):
    gain, own = 1.0, jax.random.fold_in(rng, 6)
    for dim, parts in pieces:
        steps = jnp.exp(jax.random.uniform(jax.random.fold_in(own, dim), (parts,), jnp.float32, low / len(pieces), largest / len(pieces)))
        gain = gain * jnp.repeat(steps, extent[dim] // parts).reshape([-1 if axis == dim else 1 for axis in range(len(extent))])
    return gain


def noise(stream_key, extent, width, reach, cuts=(), held_as=jnp.bfloat16):
    factor_of = level_of(stream_key, extent, cuts, -0.22, 0.18) if cuts else 1.0
    result = jax.random.normal(stream_key, extent, jnp.float32) * width * factor_of
    return jnp.minimum(jnp.maximum(result, -reach), reach).astype(held_as)


def setup_inputs(seed: int = 0) -> dict:
    arg_keys = jax.random.split(jax.random.key(seed), 8)
    return {
        "tokens": noise(arg_keys[0], (TOKENS, D), 1.0, 6.0, ((0, 32),)),
        "routes": draw_routes(jax.random.fold_in(arg_keys[7], 71), 0),
        "router_gates": set_ends(jax.random.randint(arg_keys[2], (TOKENS, TOP), 1024, 32768), jax.random.fold_in(arg_keys[2], 1), 1024, 32767).astype(jnp.int32),
        "hidden_cotangent": noise(arg_keys[3], (TOKENS, TOP, H), 1.0, 6.0, ((0, 32),)),
        "weights": noise(arg_keys[4], (2, E, H, D), D ** -0.5, 0.109375, ((2, 8), (3, 4))),
        "first_moment": noise(arg_keys[5], (2, E, H, D), 1.0, 6.0, ((2, 8), (3, 4))),
        "second_moment": jnp.clip(jnp.exp(math.log(4.0) - 2.0794415 * jax.random.uniform(arg_keys[6], (2, E, H, D), jnp.float32) ** level_of(arg_keys[6], (2, E, H, D), ((2, 8), (3, 4)), -0.2, 0.2)), 0.5, 4.0).astype(jnp.bfloat16),
    }


gate_unit = 32768.0
loss_scale = 16.0
beta_one = 0.9
beta_two = 0.95
step_size = 0.001
adam_eps = 1e-08

def swiglu_backward(slot_rows, upstream, pair_weights):
    pair_float = pair_weights.astype(jnp.float32)
    projected = jnp.einsum('rd,ahd->rah', slot_rows.astype(jnp.float32), pair_float)
    pre_gate = projected[:, 0]
    pre_up = projected[:, 1]
    sigmoid_gate = jax.nn.sigmoid(pre_gate)
    upstream_float = upstream.astype(jnp.float32)
    grad_up = (upstream_float * pre_gate * sigmoid_gate).astype(jnp.bfloat16)
    grad_gate = (upstream_float * pre_up * sigmoid_gate * (1.0 + pre_gate * (1.0 - sigmoid_gate))).astype(jnp.bfloat16)
    paired = jnp.stack([grad_gate, grad_up], axis=1)
    backward = jnp.einsum('rah,ahd->rd', paired.astype(jnp.float32), pair_float).astype(jnp.bfloat16)
    return (backward, paired)

def reference(tokens, routes, router_gates, hidden_cotangent, weights, first_moment, second_moment):
    token_total = tokens.shape[0]
    model_width = tokens.shape[1]
    experts = weights.shape[1]
    hidden_units = weights.shape[2]
    blocks = token_total // TOK
    slot_count = N_EXPERT * CAP
    routings = token_total * TOP
    flat_route = routes.reshape(blocks, TOK * TOP)
    onehot = (flat_route[:, :, None] == jnp.arange(experts, dtype=jnp.int32)[None, None, :]).astype(jnp.int32)
    position = lax.optimization_barrier(jnp.sum((jnp.cumsum(onehot, axis=1) - onehot) * onehot, axis=2))
    block_ids = jnp.arange(blocks, dtype=jnp.int32)
    source = block_ids % N_EXPERT
    group_of = block_ids // N_EXPERT
    target = (group_of[:, None] * experts + flat_route) * slot_count + source[:, None] * CAP + position
    routing_ids = jnp.arange(routings, dtype=jnp.int32)
    slot_table = jnp.full((N_DP * experts * slot_count,), routings, jnp.int32)
    slot_table = slot_table.at[target.reshape(-1)].set(routing_ids).reshape(N_DP, experts, slot_count)
    gate_factor = router_gates.astype(jnp.float32) / gate_unit
    scaled = (gate_factor[:, :, None] * hidden_cotangent.astype(jnp.float32)).astype(jnp.bfloat16)
    scaled = scaled.reshape(routings, hidden_units)

    def per_expert(routed, expert_index):
        pair_weights = lax.dynamic_index_in_dim(weights, expert_index, 1, keepdims=False)

        def per_group(carried, group_index):
            routed_all, grad_total = carried
            slot_ids = slot_table[group_index, expert_index]
            filled = slot_ids < routings
            token_index = jnp.where(filled, slot_ids // TOP, 0).astype(jnp.int32)
            slot_rows = jnp.where(filled[:, None], tokens[token_index], jnp.zeros((), jnp.bfloat16))
            upstream = jnp.where(filled[:, None], scaled[jnp.minimum(slot_ids, routings - 1)], jnp.zeros((), jnp.bfloat16))
            backward, paired = swiglu_backward(slot_rows, upstream, pair_weights)
            partial_sum = jnp.einsum('rah,rd->ahd', paired.astype(jnp.float32), slot_rows.astype(jnp.float32))
            rounded = lax.optimization_barrier(partial_sum.astype(jnp.bfloat16)).astype(jnp.float32)
            routed_all = routed_all.at[slot_ids].set(backward, mode='drop')
            return ((routed_all, grad_total + rounded), None)
        start_sum = jnp.zeros((2, hidden_units, model_width), jnp.float32)
        (routed, grad_total), _ = lax.scan(per_group, (routed, start_sum), jnp.arange(N_DP, dtype=jnp.int32))
        gradient = grad_total / loss_scale
        first_old = lax.dynamic_index_in_dim(first_moment, expert_index, 1, keepdims=False).astype(jnp.float32)
        second_old = lax.dynamic_index_in_dim(second_moment, expert_index, 1, keepdims=False).astype(jnp.float32)
        moment_one = beta_one * first_old + (1.0 - beta_one) * gradient
        moment_two = beta_two * second_old + (1.0 - beta_two) * gradient * gradient
        updated = pair_weights.astype(jnp.float32) - step_size * moment_one / (jnp.sqrt(moment_two) + adam_eps)
        return (routed, (updated.astype(jnp.bfloat16), moment_one.astype(jnp.bfloat16), moment_two.astype(jnp.bfloat16)))
    start_routed = jnp.zeros((routings, model_width), jnp.bfloat16)
    routed, results = lax.scan(per_expert, start_routed, jnp.arange(experts, dtype=jnp.int32))
    new_weights = jnp.swapaxes(results[0], 0, 1)
    new_first = jnp.swapaxes(results[1], 0, 1)
    new_second = jnp.swapaxes(results[2], 0, 1)
    token_grads = lax.optimization_barrier(jnp.sum(routed.reshape(token_total, TOP, model_width).astype(jnp.float32), axis=1)).astype(jnp.bfloat16)
    return (token_grads, new_weights, new_first, new_second)
```

```python
import jax
import jax.numpy as jnp
from jax import lax
from jax.experimental import pallas as pl
from jax.experimental.pallas import tpu as pltpu
from jax.sharding import PartitionSpec as P

gate_unit = 32768.0
loss_scale = 16.0
beta_one = 0.9
beta_two = 0.95
step_size = 0.001
adam_eps = 1e-08


def slot_targets(flat_route, capacity):
    count = flat_route.shape[-1]
    order = jnp.arange(count, dtype=jnp.int32)
    earlier = order[None, :] < order[:, None]
    same = flat_route[:, None] == flat_route[None, :]
    position = jnp.sum((same & earlier).astype(jnp.int32), axis=-1)
    return flat_route * capacity + position


def after(value, *others):
    return lax.optimization_barrier((value, *others))[0]


def adam_step(summed, old, first_old, second_old, *refs):
    f32 = jnp.float32
    weights_out, first_out, second_out = refs[-3:]
    gradient = summed[...].astype(f32) / loss_scale
    moment_one = beta_one * first_old[...].astype(f32) + (1.0 - beta_one) * gradient
    moment_two = beta_two * second_old[0, 0].astype(f32) + (1.0 - beta_two) * gradient * gradient
    updated = old[...].astype(f32) - step_size * moment_one / (jnp.sqrt(moment_two) + adam_eps)
    weights_out[0, 0] = updated.astype(weights_out.dtype)
    first_out[0, 0] = moment_one.astype(first_out.dtype)
    second_out[0, 0] = moment_two.astype(second_out.dtype)


def adam(index, summed, old, first_old, second_old, *results):
    rows, width = old.shape
    sources, _, part, _ = second_old.shape
    flat = pl.BlockSpec((part, width), lambda i: (i, 0))
    second = pl.BlockSpec((1, 1, part, width), lambda i: (i, index, 0, 0))
    out = pl.BlockSpec((1, 1, part, width), lambda i: (index, 0, i, 0))
    shape = jax.ShapeDtypeStruct((2, 1, rows, width), old.dtype)
    return pl.pallas_call(
        adam_step,
        grid=(sources,),
        in_specs=[flat] * 3 + [second] + [pl.BlockSpec(memory_space=pl.ANY)] * len(results),
        out_specs=[out] * 3,
        out_shape=[shape] * 3,
        input_output_aliases={4 + i: i for i in range(len(results))},
        cost_estimate=pl.CostEstimate(
            flops=20 * old.size, bytes_accessed=14 * old.size, transcendentals=2 * old.size
        ),
        compiler_params=pltpu.CompilerParams(vmem_limit_bytes=60 * 1024 * 1024),
    )(summed, old, first_old, second_old, *results)


def per_device(
    tokens, routes, router_gates, hidden_cotangent, weights, first_moment, second_moment
):
    row_count, model_width = tokens.shape
    per_token = routes.shape[1]
    hidden_units = hidden_cotangent.shape[2]
    experts = weights.shape[1]
    capacity = 3 * row_count * per_token // (2 * experts)
    routings = row_count * per_token
    bf16 = jnp.bfloat16
    f32 = jnp.float32
    half = experts // 2
    mine = lax.axis_index("expert")
    side = mine // half
    local = mine % half
    swap = [(i, (i + half) % experts) for i in range(experts)]

    def shift(value, step):
        if step % half == 0:
            return value
        pairs = [(i, i // half * half + (i + step) % half) for i in range(experts)]
        return lax.ppermute(value, "expert", pairs)

    def slot_ids(of_side):
        expert = of_side * half + (local + jnp.arange(half, dtype=jnp.int32)) % half
        return expert[:, None] * capacity + jnp.arange(capacity, dtype=jnp.int32)[None, :]

    def to_owners(part):
        return lax.all_to_all(part, "expert", split_axis=0, concat_axis=1, tiled=True)[0]

    def over_dp(part):
        return lax.all_gather(part, "dp", axis=1, tiled=True)

    other_tokens = lax.ppermute(tokens, "expert", swap)
    other_routes = lax.ppermute(routes, "expert", swap)

    owned_gate = to_owners(weights[0])
    gate_factor = router_gates.astype(f32) / gate_unit
    scaled = (gate_factor[:, :, None] * hidden_cotangent.astype(f32)).astype(bf16)
    scaled = scaled.reshape(routings, hidden_units)
    target = slot_targets(routes.reshape(-1), capacity)
    other_target = slot_targets(other_routes.reshape(-1), capacity)
    near_ids = slot_ids(side)
    far_ids = slot_ids(1 - side)

    def pick_grads(ids, scaled):
        chosen = (target[None, :] == ids.reshape(-1)[:, None]).astype(bf16)
        picked = jnp.dot(chosen, scaled, preferred_element_type=f32).astype(bf16)
        return picked.reshape(half, capacity, hidden_units)

    far_grads = lax.ppermute(pick_grads(far_ids, after(scaled, owned_gate)), "expert", swap)
    grads_out = jnp.concatenate([far_grads, pick_grads(near_ids, scaled)], axis=1)
    grads_in = [shift(grads_out[s], s) for s in range(half)]
    upstream = jnp.swapaxes(jnp.stack(grads_in).reshape(half, 2, capacity, hidden_units), 0, 1)

    def pick_matrix(chosen_target):
        by_token = chosen_target.reshape(row_count, per_token)
        hit = by_token[None, :, :] == near_ids.reshape(-1)[:, None, None]
        return jnp.any(hit, axis=2).astype(bf16)

    near_pick = pick_matrix(target)
    other_pick = pick_matrix(other_target)

    def send_rows(picker, rows):
        picked = jnp.dot(picker, rows, preferred_element_type=f32).astype(bf16)
        picked = picked.reshape(half, capacity, model_width)
        return [shift(picked[s], s) for s in range(half)]

    near_rows = send_rows(near_pick, tokens)
    other_tokens = after(other_tokens, other_routes, *near_rows[1:])
    full_gate = over_dp(after(owned_gate, other_tokens))
    owned_up = to_owners(after(weights[1], owned_gate, other_tokens))
    far_rows = send_rows(other_pick, other_tokens)
    full_up = over_dp(after(owned_up, far_grads, *far_rows[1:]))
    flat_rows = jnp.concatenate(far_rows + near_rows, axis=0)

    first_gate = to_owners(after(first_moment[0], owned_up))
    first_up = to_owners(after(first_moment[1], first_gate))

    slots = flat_rows.shape[0]
    pre_gate = jnp.einsum("rd,hd->rh", flat_rows, full_gate, preferred_element_type=f32)
    pre_up = jnp.einsum("rd,hd->rh", flat_rows, full_up, preferred_element_type=f32)
    sigmoid_gate = jax.nn.sigmoid(pre_gate)
    upstream = upstream.reshape(slots, hidden_units).astype(f32)
    grad_up = (upstream * pre_gate * sigmoid_gate).astype(bf16)
    grad_gate = (upstream * pre_up * sigmoid_gate * (1.0 + pre_gate * (1.0 - sigmoid_gate))).astype(
        bf16
    )

    def weight_grad(grads, *earlier):
        total = jnp.einsum("rh,rd->hd", grads, flat_rows, preferred_element_type=f32)
        total = after(total.astype(bf16), *earlier)
        return lax.psum_scatter(total, "dp", scatter_dimension=1, tiled=True)

    up_sum = weight_grad(after(grad_up, first_gate))
    backward = (
        jnp.dot(grad_gate, full_gate, preferred_element_type=f32)
        + jnp.dot(grad_up, full_up, preferred_element_type=f32)
    ).astype(bf16)
    by_half = backward.reshape(2, half, capacity, model_width)
    far_back = [shift(by_half[0, s], -s) for s in range(half)]
    near_back = [shift(by_half[1, s], -s) for s in range(half)]
    gate_sum = weight_grad(after(grad_gate, backward), first_up, *far_back[1:])
    owned_second = lax.all_to_all(
        after(second_moment, first_up), "expert", split_axis=1, concat_axis=0
    )

    def combine(picker, rows):
        rows = jnp.concatenate(rows, axis=0)
        return jnp.einsum("st,sd->td", picker, rows, preferred_element_type=f32)

    far_sum = after(combine(other_pick, far_back).astype(bf16), owned_second)
    far_sum = lax.ppermute(far_sum, "expert", swap)
    results = adam(1, up_sum, owned_up, first_up, owned_second)
    results = adam(0, gate_sum, owned_gate, first_gate, owned_second, *results)
    near_back[1] = after(near_back[1], *results)
    token_grads = (combine(near_pick, near_back) + far_sum.astype(f32)).astype(bf16)
    return (token_grads, *results)


def solution(mesh):
    placed = (
        P(("dp", "expert"), None),
        P(("dp", "expert"), None),
        P(("dp", "expert"), None),
        P(("dp", "expert"), None, None),
        P(None, None, "expert", "dp"),
        P(None, None, "expert", "dp"),
        P(None, None, "expert", "dp"),
    )
    return jax.shard_map(
        per_device,
        mesh=mesh,
        in_specs=placed,
        out_specs=(
            P(("dp", "expert"), None),
            P(None, "expert", None, "dp"),
            P(None, "expert", None, "dp"),
            P(None, "expert", None, "dp"),
        ),
        check_vma=False,
    )
```

```python
import jax
import jax.numpy as jnp
from jax import lax
from jax.experimental import pallas as pl
from jax.experimental.pallas import tpu as pltpu
from jax.sharding import PartitionSpec as P

gate_unit = 32768.0
loss_scale = 16.0
beta_one = 0.9
beta_two = 0.95
step_size = 0.001
adam_eps = 1e-08
bf16 = jnp.bfloat16
f32 = jnp.float32
vmem_bytes = 32 * 1024 * 1024


def after(value, *others):
    return lax.optimization_barrier((value, *others))[0]


def tile_of(extent):
    return 256 if extent % 256 == 0 else extent


def whole(shape):
    return pl.BlockSpec(shape, lambda *_: (0,) * len(shape))


def run(body, place, grid, in_specs, out_specs, out_shape, *operands):
    return pl.pallas_call(
        body,
        grid_spec=pltpu.PrefetchScalarGridSpec(
            num_scalar_prefetch=1, grid=grid, in_specs=in_specs, out_specs=out_specs
        ),
        out_shape=out_shape,
        compiler_params=pltpu.CompilerParams(vmem_limit_bytes=vmem_bytes),
    )(place, *operands)


def columns(place, k, width, start=0, size=None):
    first = pl.multiple_of((place[0] ^ k) * width + start, 128)
    return pl.ds(first, width if size is None else size)


def project(place, rows, weights):
    total = None
    for k, piece in enumerate(weights):
        term = lax.dot_general(
            rows[:, columns(place, k, piece.shape[1])],
            piece[...],
            (((1,), (1,)), ((), ())),
            preferred_element_type=f32,
        )
        total = term if total is None else total + term
    return total


def forward_gate(place, blocks, upstream, gate):
    pieces, hidden = len(gate), gate[0].shape[0]
    width = gate[0].shape[1] * pieces
    count = sum(block.shape[0] for block in blocks)
    tile = tile_of(hidden)

    def body(place, *refs):
        block_refs, refs = refs[: len(blocks)], refs[len(blocks) :]
        up_ref, gate_refs = refs[0], refs[1 : 1 + pieces]
        rows, grad_up, factor = refs[1 + pieces :]

        @pl.when(pl.program_id(0) == 0)
        def _():
            first = 0
            for block in block_refs:
                rows[first : first + block.shape[0], :] = block[...]
                first += block.shape[0]

        pre_gate = project(place, rows, gate_refs)
        sigmoid_gate = jax.nn.sigmoid(pre_gate)
        upstream = up_ref[...].astype(f32) * sigmoid_gate
        grad_up[...] = (upstream * pre_gate).astype(bf16)
        factor[...] = upstream * (1.0 + pre_gate * (1.0 - sigmoid_gate))

    part = pl.BlockSpec((count, tile), lambda i, _: (0, i))
    return run(
        body,
        place,
        (hidden // tile,),
        [whole(block.shape) for block in blocks]
        + [part]
        + [pl.BlockSpec((tile, width // pieces), lambda i, _: (i, 0))] * pieces,
        [whole((count, width)), part, part],
        [
            jax.ShapeDtypeStruct((count, width), bf16),
            jax.ShapeDtypeStruct((count, hidden), bf16),
            jax.ShapeDtypeStruct((count, hidden), f32),
        ],
        *blocks,
        upstream,
        *gate,
    )


def forward_up(place, rows, factor, up):
    pieces, hidden = len(up), up[0].shape[0]
    count, width = rows.shape
    tile = tile_of(hidden)

    def body(place, rows, factor, *refs):
        refs[-1][...] = (factor[...] * project(place, rows, refs[:-1])).astype(bf16)

    part = pl.BlockSpec((count, tile), lambda i, _: (0, i))
    return run(
        body,
        place,
        (hidden // tile,),
        [whole((count, width)), part]
        + [pl.BlockSpec((tile, width // pieces), lambda i, _: (i, 0))] * pieces,
        part,
        jax.ShapeDtypeStruct((count, hidden), bf16),
        rows,
        factor,
        *up,
    )


def weight_grads(place, grads, rows, pieces):
    count, hidden = grads.shape
    width = rows.shape[1] // pieces
    tile = tile_of(hidden)

    def body(place, grads, rows, *outs):
        for k, out in enumerate(outs):
            out[...] = lax.dot_general(
                grads[...],
                rows[:, columns(place, k, width)],
                (((0,), (0,)), ((), ())),
                preferred_element_type=f32,
            ).astype(bf16)

    return run(
        body,
        place,
        (hidden // tile,),
        [pl.BlockSpec((count, tile), lambda i, _: (0, i)), whole(rows.shape)],
        [pl.BlockSpec((tile, width), lambda i, _: (i, 0))] * pieces,
        [jax.ShapeDtypeStruct((hidden, width), bf16)] * pieces,
        grads,
        rows,
    )


def input_grads(place, grad_gate, grad_up, gate, up, block_rows):
    count, hidden = grad_gate.shape
    pieces, width = len(gate), gate[0].shape[1]
    tile = tile_of(width)
    blocks = count // block_rows

    def body(place, grad_gate, grad_up, *refs):
        start = pl.program_id(0) * tile
        for k in range(pieces):
            total = jnp.dot(grad_gate[...], refs[k][...], preferred_element_type=f32)
            total += jnp.dot(grad_up[...], refs[pieces + k][...], preferred_element_type=f32)
            total = total.astype(bf16)
            for b, out in enumerate(refs[2 * pieces :]):
                out[:, columns(place, k, width, start, tile)] = total[
                    b * block_rows : (b + 1) * block_rows
                ]

    return run(
        body,
        place,
        (width // tile,),
        [whole((count, hidden))] * 2
        + [pl.BlockSpec((hidden, tile), lambda i, _: (0, i))] * (2 * pieces),
        [whole((block_rows, width * pieces))] * blocks,
        [jax.ShapeDtypeStruct((block_rows, width * pieces), bf16)] * blocks,
        grad_gate,
        grad_up,
        *gate,
        *up,
    )


def adam(index, parts, old, first_old, second_old, *results):
    rows, width = old.shape
    sources, _, part, _ = second_old.shape
    flat = pl.BlockSpec((part, width), lambda i: (i, 0))
    moment = pl.BlockSpec((1, 1, part, width), lambda i: (i, index, 0, 0))
    out = pl.BlockSpec((1, 1, part, width), lambda i: (index, 0, i, 0))
    shape = jax.ShapeDtypeStruct((2, 1, rows, width), old.dtype)
    count = len(parts)

    def body(*refs):
        old_ref, first_ref, second_ref = refs[count : count + 3]
        weights_out, first_out, second_out = refs[-3:]
        gradient = refs[0][...].astype(f32)
        for ref in refs[1:count]:
            gradient += ref[...].astype(f32)
        gradient = gradient / loss_scale
        moment_one = beta_one * first_ref[0, 0].astype(f32) + (1.0 - beta_one) * gradient
        moment_two = (
            beta_two * second_ref[0, 0].astype(f32) + (1.0 - beta_two) * gradient * gradient
        )
        updated = old_ref[...].astype(f32) - step_size * moment_one / (
            jnp.sqrt(moment_two) + adam_eps
        )
        weights_out[0, 0] = updated.astype(bf16)
        first_out[0, 0] = moment_one.astype(bf16)
        second_out[0, 0] = moment_two.astype(bf16)

    return pl.pallas_call(
        body,
        grid=(sources,),
        in_specs=[flat] * (count + 1)
        + [moment] * 2
        + [pl.BlockSpec(memory_space=pl.ANY)] * len(results),
        out_specs=[out] * 3,
        out_shape=[shape] * 3,
        input_output_aliases={count + 3 + i: i for i in range(len(results))},
        compiler_params=pltpu.CompilerParams(vmem_limit_bytes=vmem_bytes),
    )(*parts, old, first_old, second_old, *results)


def slot_targets(flat_route, capacity):
    count = flat_route.shape[-1]
    order = jnp.arange(count, dtype=jnp.int32)
    earlier = order[None, :] < order[:, None]
    same = flat_route[:, None] == flat_route[None, :]
    position = jnp.sum((same & earlier).astype(jnp.int32), axis=-1)
    return flat_route * capacity + position


def per_device(
    tokens, routes, router_gates, hidden_cotangent, weights, first_moment, second_moment
):
    row_count, model_width = tokens.shape
    per_token = routes.shape[1]
    hidden_units = hidden_cotangent.shape[2]
    experts = weights.shape[1]
    pieces = model_width // weights.shape[3]
    capacity = 3 * row_count * per_token // (2 * experts)
    routings = row_count * per_token
    half = experts // 2
    mine = lax.axis_index("expert")
    side = mine // half
    local = mine % half
    place = lax.axis_index("dp").astype(jnp.int32).reshape(1)
    swap = [(i, (i + half) % experts) for i in range(experts)]

    def shift(value, step):
        if step % half == 0:
            return value
        pairs = [(i, i // half * half + (i + step) % half) for i in range(experts)]
        return lax.ppermute(value, "expert", pairs)

    def across(value, k):
        return lax.ppermute(value, "dp", [(i, i ^ k) for i in range(pieces)])

    def slot_ids(of_side):
        expert = of_side * half + (local + jnp.arange(half, dtype=jnp.int32)) % half
        return expert[:, None] * capacity + jnp.arange(capacity, dtype=jnp.int32)[None, :]

    def to_owners(part, *earlier):
        by_owner = after(jnp.swapaxes(part, 0, 1), *earlier) if earlier else jnp.swapaxes(part, 0, 1)
        return lax.all_to_all(by_owner, "expert", split_axis=0, concat_axis=0, tiled=True)

    def along_x(part):
        return [across(part, k) for k in range(2, pieces, 2)]

    def both_cores(parts):
        return [piece for one in parts for piece in (one, across(one, 1))]

    def scatter(totals, *earlier):
        terms = [totals[0], across(totals[1], 1)]
        for k in range(2, pieces, 2):
            pair = totals[k].astype(f32) + across(totals[k + 1], 1).astype(f32)
            terms.append(across(after(pair.astype(bf16), *earlier), k))
        return terms

    other_tokens = lax.ppermute(tokens, "expert", swap)
    other_routes = lax.ppermute(routes, "expert", swap)

    gate_factor = router_gates.astype(f32) / gate_unit
    scaled = (gate_factor[:, :, None] * hidden_cotangent.astype(f32)).astype(bf16)
    scaled = scaled.reshape(routings, hidden_units)
    target = slot_targets(routes.reshape(-1), capacity)
    near_ids = slot_ids(side)
    far_ids = slot_ids(1 - side)

    def pick_grads(ids):
        chosen = (target[None, :] == ids.reshape(-1)[:, None]).astype(bf16)
        picked = jnp.dot(chosen, scaled, preferred_element_type=f32).astype(bf16)
        return picked.reshape(half, capacity, hidden_units)

    far_grads = lax.ppermute(pick_grads(far_ids), "expert", swap)

    def pick_matrix(chosen_target):
        by_token = chosen_target.reshape(row_count, per_token)
        hit = by_token[None, :, :] == near_ids.reshape(-1)[:, None, None]
        return jnp.any(hit, axis=2).astype(bf16)

    def send_rows(picker, rows):
        picked = jnp.dot(picker, rows, preferred_element_type=f32).astype(bf16)
        picked = picked.reshape(half, capacity, model_width)
        return [shift(picked[s], s) for s in range(half)]

    near_pick = pick_matrix(target)
    near_rows = send_rows(near_pick, tokens)
    other_tokens = after(other_tokens, other_routes, far_grads, *near_rows[1:])
    other_pick = pick_matrix(slot_targets(other_routes.reshape(-1), capacity))
    far_rows = send_rows(other_pick, other_tokens)
    grads_out = jnp.concatenate([far_grads, pick_grads(near_ids)], axis=1)
    grads_in = [shift(grads_out[s], s) for s in range(half)]

    owned = after(to_owners(weights, other_tokens), *far_rows[1:], *grads_in[1:])
    owned_gate = owned[:, 0].reshape(hidden_units, -1)
    owned_up = owned[:, 1].reshape(hidden_units, -1)
    owned_first = to_owners(first_moment, owned)

    gate_x = along_x(owned_gate)
    up_x = along_x(after(owned_up, *gate_x))
    gate = both_cores([owned_gate] + gate_x)
    up = both_cores([owned_up] + up_x)
    upstream = jnp.swapaxes(jnp.stack(grads_in).reshape(half, 2, capacity, hidden_units), 0, 1)
    upstream = upstream.reshape(2 * half * capacity, hidden_units)

    blocks = far_rows + near_rows
    joined = capacity % 16 != 0
    if joined:
        blocks = [jnp.concatenate(blocks, axis=0)]
    rows, grad_up, factor = forward_gate(place, blocks, upstream, gate)
    up_totals = weight_grads(place, grad_up, rows, pieces)
    up_terms = scatter(up_totals)
    owned_second = to_owners(second_moment, owned_first, up_totals[0])
    grad_gate = forward_up(place, rows, after(factor, owned_first), up)
    back = input_grads(
        place, grad_gate, grad_up, gate, up, rows.shape[0] if joined else capacity
    )
    if joined:
        back = [back[0][i * capacity : (i + 1) * capacity] for i in range(2 * half)]
    far_back = [shift(back[s], -s) for s in range(half)]
    near_back = [shift(after(back[half + s], *far_back[1:]), -s) for s in range(half)]
    gate_totals = weight_grads(place, after(grad_gate, *back), rows, pieces)
    gate_terms = scatter(gate_totals, *up_terms)

    def combine(picker, parts):
        parts = jnp.concatenate(parts, axis=0)
        return jnp.einsum("st,sd->td", picker, parts, preferred_element_type=f32)

    far_sum = after(combine(other_pick, far_back).astype(bf16), owned_second, *up_terms)
    far_sum = lax.ppermute(far_sum, "expert", swap)
    results = adam(1, up_terms, owned_up, owned_first, owned_second)
    results = adam(0, gate_terms, owned_gate, owned_first, owned_second, *results)
    near_back[1:] = [after(block, *results) for block in near_back[1:]]
    near_sum = combine(near_pick, near_back)
    token_grads = (near_sum + far_sum.astype(f32)).astype(bf16)
    return (token_grads, *results)


def solution(mesh):
    placed = (
        P(("dp", "expert"), None),
        P(("dp", "expert"), None),
        P(("dp", "expert"), None),
        P(("dp", "expert"), None, None),
        P(None, None, "expert", "dp"),
        P(None, None, "expert", "dp"),
        P(None, None, "expert", "dp"),
    )
    return jax.shard_map(
        per_device,
        mesh=mesh,
        in_specs=placed,
        out_specs=(
            P(("dp", "expert"), None),
            P(None, "expert", None, "dp"),
            P(None, "expert", None, "dp"),
            P(None, "expert", None, "dp"),
        ),
        check_vma=False,
    )
```

```python
import jax
import jax.numpy as jnp
from jax import lax
from jax.experimental import pallas as pl
from jax.experimental.pallas import tpu as pltpu
from jax.sharding import PartitionSpec as P

gate_unit = 32768.0
loss_scale = 16.0
beta_one = 0.9
beta_two = 0.95
step_size = 0.001
adam_eps = 1e-08
bf16 = jnp.bfloat16
f32 = jnp.float32
vmem_bytes = 32 * 1024 * 1024


def after(value, *others):
    return lax.optimization_barrier((value, *others))[0]


def tile_of(extent):
    return 256 if extent % 256 == 0 else extent


def whole(shape):
    return pl.BlockSpec(shape, lambda *_: (0,) * len(shape))


def run(body, place, grid, in_specs, out_specs, out_shape, *operands):
    return pl.pallas_call(
        body,
        grid_spec=pltpu.PrefetchScalarGridSpec(
            num_scalar_prefetch=1, grid=grid, in_specs=in_specs, out_specs=out_specs
        ),
        out_shape=out_shape,
        compiler_params=pltpu.CompilerParams(vmem_limit_bytes=vmem_bytes),
    )(place, *operands)


def columns(place, k, width, start=0, size=None):
    first = pl.multiple_of((place[0] ^ k) * width + start, 128)
    return pl.ds(first, width if size is None else size)


def project(place, rows, weights):
    total = None
    for k, piece in enumerate(weights):
        term = lax.dot_general(
            rows[:, columns(place, k, piece.shape[1])],
            piece[...],
            (((1,), (1,)), ((), ())),
            preferred_element_type=f32,
        )
        total = term if total is None else total + term
    return total


def forward_gate(place, blocks, upstream, gate):
    pieces, hidden = len(gate), gate[0].shape[0]
    width = gate[0].shape[1] * pieces
    count = sum(block.shape[0] for block in blocks)
    tile = tile_of(hidden)

    def body(place, *refs):
        block_refs, refs = refs[: len(blocks)], refs[len(blocks) :]
        up_ref, gate_refs = refs[0], refs[1 : 1 + pieces]
        rows, grad_up, factor = refs[1 + pieces :]

        @pl.when(pl.program_id(0) == 0)
        def _():
            first = 0
            for block in block_refs:
                rows[first : first + block.shape[0], :] = block[...]
                first += block.shape[0]

        pre_gate = project(place, rows, gate_refs)
        sigmoid_gate = jax.nn.sigmoid(pre_gate)
        upstream = up_ref[...].astype(f32) * sigmoid_gate
        grad_up[...] = (upstream * pre_gate).astype(bf16)
        factor[...] = upstream * (1.0 + pre_gate * (1.0 - sigmoid_gate))

    part = pl.BlockSpec((count, tile), lambda i, _: (0, i))
    return run(
        body,
        place,
        (hidden // tile,),
        [whole(block.shape) for block in blocks]
        + [part]
        + [pl.BlockSpec((tile, width // pieces), lambda i, _: (i, 0))] * pieces,
        [whole((count, width)), part, part],
        [
            jax.ShapeDtypeStruct((count, width), bf16),
            jax.ShapeDtypeStruct((count, hidden), bf16),
            jax.ShapeDtypeStruct((count, hidden), f32),
        ],
        *blocks,
        upstream,
        *gate,
    )


def forward_up(place, rows, factor, up):
    pieces, hidden = len(up), up[0].shape[0]
    count, width = rows.shape
    tile = tile_of(hidden)

    def body(place, rows, factor, *refs):
        refs[-1][...] = (factor[...] * project(place, rows, refs[:-1])).astype(bf16)

    part = pl.BlockSpec((count, tile), lambda i, _: (0, i))
    return run(
        body,
        place,
        (hidden // tile,),
        [whole((count, width)), part]
        + [pl.BlockSpec((tile, width // pieces), lambda i, _: (i, 0))] * pieces,
        part,
        jax.ShapeDtypeStruct((count, hidden), bf16),
        rows,
        factor,
        *up,
    )


def weight_grads(place, grads, rows, pieces):
    count, hidden = grads.shape
    width = rows.shape[1] // pieces
    tile = tile_of(hidden)

    def body(place, grads, rows, *outs):
        for k, out in enumerate(outs):
            out[...] = lax.dot_general(
                grads[...],
                rows[:, columns(place, k, width)],
                (((0,), (0,)), ((), ())),
                preferred_element_type=f32,
            ).astype(bf16)

    return run(
        body,
        place,
        (hidden // tile,),
        [pl.BlockSpec((count, tile), lambda i, _: (0, i)), whole(rows.shape)],
        [pl.BlockSpec((tile, width), lambda i, _: (i, 0))] * pieces,
        [jax.ShapeDtypeStruct((hidden, width), bf16)] * pieces,
        grads,
        rows,
    )


def input_grads(place, grad_gate, grad_up, gate, up, block_rows):
    count, hidden = grad_gate.shape
    pieces, width = len(gate), gate[0].shape[1]
    tile = tile_of(width)
    blocks = count // block_rows

    def body(place, grad_gate, grad_up, *refs):
        start = pl.program_id(0) * tile
        for k in range(pieces):
            total = jnp.dot(grad_gate[...], refs[k][...], preferred_element_type=f32)
            total += jnp.dot(grad_up[...], refs[pieces + k][...], preferred_element_type=f32)
            total = total.astype(bf16)
            for b, out in enumerate(refs[2 * pieces :]):
                out[:, columns(place, k, width, start, tile)] = total[
                    b * block_rows : (b + 1) * block_rows
                ]

    return run(
        body,
        place,
        (width // tile,),
        [whole((count, hidden))] * 2
        + [pl.BlockSpec((hidden, tile), lambda i, _: (0, i))] * (2 * pieces),
        [whole((block_rows, width * pieces))] * blocks,
        [jax.ShapeDtypeStruct((block_rows, width * pieces), bf16)] * blocks,
        grad_gate,
        grad_up,
        *gate,
        *up,
    )


def adam(index, parts, old, moments, *results):
    rows, width = old.shape
    sources, _, _, part, _ = moments.shape
    flat = pl.BlockSpec((part, width), lambda i: (i, 0))
    moment = pl.BlockSpec((1, 2, 1, part, width), lambda i: (i, 0, index, 0, 0))
    out = pl.BlockSpec((1, 1, part, width), lambda i: (index, 0, i, 0))
    shape = jax.ShapeDtypeStruct((2, 1, rows, width), old.dtype)
    count = len(parts)

    def body(*refs):
        old_ref, moments_ref = refs[count : count + 2]
        weights_out, first_out, second_out = refs[-3:]
        gradient = refs[0][...].astype(f32)
        for ref in refs[1:count]:
            gradient += ref[...].astype(f32)
        gradient = gradient / loss_scale
        moment_one = beta_one * moments_ref[0, 0, 0].astype(f32) + (1.0 - beta_one) * gradient
        moment_two = (
            beta_two * moments_ref[0, 1, 0].astype(f32) + (1.0 - beta_two) * gradient * gradient
        )
        updated = old_ref[...].astype(f32) - step_size * moment_one / (
            jnp.sqrt(moment_two) + adam_eps
        )
        weights_out[0, 0] = updated.astype(bf16)
        first_out[0, 0] = moment_one.astype(bf16)
        second_out[0, 0] = moment_two.astype(bf16)

    return pl.pallas_call(
        body,
        grid=(sources,),
        in_specs=[flat] * (count + 1)
        + [moment]
        + [pl.BlockSpec(memory_space=pl.ANY)] * len(results),
        out_specs=[out] * 3,
        out_shape=[shape] * 3,
        input_output_aliases={count + 2 + i: i for i in range(len(results))},
        compiler_params=pltpu.CompilerParams(vmem_limit_bytes=vmem_bytes),
    )(*parts, old, moments, *results)


def slot_targets(flat_route, capacity):
    count = flat_route.shape[-1]
    order = jnp.arange(count, dtype=jnp.int32)
    earlier = order[None, :] < order[:, None]
    same = flat_route[:, None] == flat_route[None, :]
    position = jnp.sum((same & earlier).astype(jnp.int32), axis=-1)
    return flat_route * capacity + position


def per_device(
    tokens, routes, router_gates, hidden_cotangent, weights, first_moment, second_moment
):
    row_count, model_width = tokens.shape
    per_token = routes.shape[1]
    hidden_units = hidden_cotangent.shape[2]
    experts = weights.shape[1]
    pieces = model_width // weights.shape[3]
    capacity = 3 * row_count * per_token // (2 * experts)
    routings = row_count * per_token
    half = experts // 2
    mine = lax.axis_index("expert")
    side = mine // half
    local = mine % half
    place = lax.axis_index("dp").astype(jnp.int32).reshape(1)
    swap = [(i, (i + half) % experts) for i in range(experts)]

    def shift(value, step):
        if step % half == 0:
            return value
        pairs = [(i, i // half * half + (i + step) % half) for i in range(experts)]
        return lax.ppermute(value, "expert", pairs)

    def across(value, k):
        return lax.ppermute(value, "dp", [(i, i ^ k) for i in range(pieces)])

    def slot_ids(of_side):
        expert = of_side * half + (local + jnp.arange(half, dtype=jnp.int32)) % half
        return expert[:, None] * capacity + jnp.arange(capacity, dtype=jnp.int32)[None, :]

    def to_owners(by_owner, *earlier):
        by_owner = after(by_owner, *earlier)
        return lax.all_to_all(by_owner, "expert", split_axis=0, concat_axis=0, tiled=True)

    def along_x(part):
        return [across(part, k) for k in range(2, pieces, 2)]

    def both_cores(parts):
        return [piece for one in parts for piece in (one, across(one, 1))]

    def core_sums(totals):
        sums = []
        for k in range(2, pieces, 2):
            pair = totals[k].astype(f32) + across(totals[k + 1], 1).astype(f32)
            sums.append(pair.astype(bf16))
        return sums

    def scatter(totals, sums):
        sums = [across(pair, 2 * (k + 1)) for k, pair in enumerate(sums)]
        return [totals[0], across(totals[1], 1)] + sums

    other_tokens = lax.ppermute(tokens, "expert", swap)
    other_routes = lax.ppermute(routes, "expert", swap)

    gate_factor = router_gates.astype(f32) / gate_unit
    scaled = (gate_factor[:, :, None] * hidden_cotangent.astype(f32)).astype(bf16)
    scaled = scaled.reshape(routings, hidden_units)
    target = slot_targets(routes.reshape(-1), capacity)
    near_ids = slot_ids(side)
    far_ids = slot_ids(1 - side)

    def pick_grads(ids):
        chosen = (target[None, :] == ids.reshape(-1)[:, None]).astype(bf16)
        picked = jnp.dot(chosen, scaled, preferred_element_type=f32).astype(bf16)
        return picked.reshape(half, capacity, hidden_units)

    far_grads = lax.ppermute(pick_grads(far_ids), "expert", swap)

    def pick_matrix(chosen_target):
        by_token = chosen_target.reshape(row_count, per_token)
        hit = by_token[None, :, :] == near_ids.reshape(-1)[:, None, None]
        return jnp.any(hit, axis=2).astype(bf16)

    def send_rows(picker, rows):
        picked = jnp.dot(picker, rows, preferred_element_type=f32).astype(bf16)
        picked = picked.reshape(half, capacity, model_width)
        return [shift(picked[s], s) for s in range(half)]

    near_pick = pick_matrix(target)
    near_rows = send_rows(near_pick, tokens)
    grads_out = jnp.concatenate([far_grads, pick_grads(near_ids)], axis=1)
    grads_in = [shift(grads_out[s], s) for s in range(half)]
    other_tokens = after(other_tokens, other_routes, *grads_in[1:], *near_rows[1:])
    other_pick = pick_matrix(slot_targets(other_routes.reshape(-1), capacity))
    far_rows = send_rows(other_pick, other_tokens)

    owned = after(to_owners(jnp.swapaxes(weights, 0, 1), other_tokens), *far_rows[1:])
    owned_gate = owned[:, 0].reshape(hidden_units, -1)
    owned_up = owned[:, 1].reshape(hidden_units, -1)
    moments = [jnp.swapaxes(moment, 0, 1) for moment in (first_moment, second_moment)]
    moments = to_owners(jnp.stack(moments, axis=1), owned)

    gate_x = along_x(owned_gate)
    up_x = along_x(after(owned_up, *gate_x))
    gate = both_cores([owned_gate] + gate_x)
    up = both_cores([owned_up] + up_x)
    upstream = jnp.swapaxes(jnp.stack(grads_in).reshape(half, 2, capacity, hidden_units), 0, 1)
    upstream = upstream.reshape(2 * half * capacity, hidden_units)

    blocks = far_rows + near_rows
    joined = capacity % 16 != 0
    if joined:
        blocks = [jnp.concatenate(blocks, axis=0)]
    rows, grad_up, factor = forward_gate(place, blocks, upstream, gate)
    up_totals = weight_grads(place, grad_up, rows, pieces)
    up_sums = core_sums(up_totals)
    up_terms = scatter(up_totals, up_sums)
    grad_gate = forward_up(place, rows, after(factor, *up_sums), up)
    back = input_grads(
        place, grad_gate, grad_up, gate, up, rows.shape[0] if joined else capacity
    )
    if joined:
        back = [back[0][i * capacity : (i + 1) * capacity] for i in range(2 * half)]
    far_back = [shift(back[s], -s) for s in range(half)]
    near_back = [shift(after(back[half + s], *far_back[1:]), -s) for s in range(half)]
    gate_totals = weight_grads(place, after(grad_gate, *back), rows, pieces)
    gate_sums = [after(pair, *up_terms) for pair in core_sums(gate_totals)]
    gate_terms = scatter(gate_totals, gate_sums)

    def combine(picker, parts):
        parts = jnp.concatenate(parts, axis=0)
        return jnp.einsum("st,sd->td", picker, parts, preferred_element_type=f32)

    far_sum = after(combine(other_pick, far_back).astype(bf16), moments, *up_terms)
    far_sum = lax.ppermute(far_sum, "expert", swap)
    results = adam(1, up_terms, owned_up, moments)
    results = adam(0, gate_terms, owned_gate, moments, *results)
    near_back[1:] = [after(block, *results) for block in near_back[1:]]
    near_sum = combine(near_pick, near_back)
    token_grads = (near_sum + far_sum.astype(f32)).astype(bf16)
    return (token_grads, *results)


def solution(mesh):
    placed = (
        P(("dp", "expert"), None),
        P(("dp", "expert"), None),
        P(("dp", "expert"), None),
        P(("dp", "expert"), None, None),
        P(None, None, "expert", "dp"),
        P(None, None, "expert", "dp"),
        P(None, None, "expert", "dp"),
    )
    return jax.shard_map(
        per_device,
        mesh=mesh,
        in_specs=placed,
        out_specs=(
            P(("dp", "expert"), None),
            P(None, "expert", None, "dp"),
            P(None, "expert", None, "dp"),
            P(None, "expert", None, "dp"),
        ),
        check_vma=False,
    )
```

```python
import jax
import jax.numpy as jnp
from jax import lax
from jax.experimental import pallas as pl
from jax.experimental.pallas import tpu as pltpu
from jax.sharding import PartitionSpec as P

gate_unit = 32768.0
loss_scale = 16.0
beta_one = 0.9
beta_two = 0.95
step_size = 0.001
adam_eps = 1e-08
bf16 = jnp.bfloat16
f32 = jnp.float32
vmem_bytes = 32 * 1024 * 1024


def after(value, *others):
    return lax.optimization_barrier((value, *others))[0]


def tile_of(extent):
    return 256 if extent % 256 == 0 else extent


def whole(shape):
    return pl.BlockSpec(shape, lambda *_: (0,) * len(shape))


def run(body, place, grid, in_specs, out_specs, out_shape, *operands):
    return pl.pallas_call(
        body,
        grid_spec=pltpu.PrefetchScalarGridSpec(
            num_scalar_prefetch=1, grid=grid, in_specs=in_specs, out_specs=out_specs
        ),
        out_shape=out_shape,
        compiler_params=pltpu.CompilerParams(vmem_limit_bytes=vmem_bytes),
    )(place, *operands)


def columns(place, k, width, start=0, size=None):
    first = pl.multiple_of((place[0] ^ k) * width + start, 128)
    return pl.ds(first, width if size is None else size)


def project(place, rows, weights):
    total = None
    for k, piece in enumerate(weights):
        term = lax.dot_general(
            rows[:, columns(place, k, piece.shape[1])],
            piece[...],
            (((1,), (1,)), ((), ())),
            preferred_element_type=f32,
        )
        total = term if total is None else total + term
    return total


def chosen_by(info, which, route_rows, route_cols, capacity, half):
    choices, count = route_rows.shape
    slot = lax.broadcasted_iota(jnp.int32, (half * capacity, 1), 0)
    number = jnp.zeros_like(slot)
    for k in range(1, half):
        number += (slot >= k * capacity).astype(jnp.int32)
    expert = info[0] + number
    expert = jnp.where(expert >= half, expert - half, expert) + which * half
    slot = (expert * capacity + slot - number * capacity).astype(f32)
    before = lax.broadcasted_iota(jnp.int32, (count, count), 0)
    before = before < lax.broadcasted_iota(jnp.int32, (count, count), 1)
    chosen = []
    for k in range(choices):
        row = route_rows[k : k + 1, :]
        position = jnp.zeros((1, count), f32)
        for other in range(k + 1):
            same = route_cols[:, other : other + 1] == row
            if other == k:
                same = same & before
            position += jnp.sum(jnp.where(same, 1.0, 0.0), axis=0, keepdims=True)
        target = row.astype(f32) * capacity + position
        chosen.append(jnp.where(target == slot, 1.0, 0.0).astype(bf16))
    return chosen


def store_blocks(refs, start, picked):
    part = picked.shape[0] // len(refs)
    for number, ref in enumerate(refs):
        ref[:, start : start + picked.shape[1]] = picked[number * part : (number + 1) * part]


def pick_near(info, routes, gates, cotangent, tokens, capacity, half):
    count, width = tokens.shape
    hidden = cotangent.shape[2]
    slots = half * capacity
    blocks = half if capacity % 16 == 0 else 1

    def body(info, route_rows, route_cols, gates, cotangent, tokens, *outs):
        for which, out in ((1 - info[1], outs[0]), (info[1], outs[1])):
            chosen = chosen_by(info, which, route_rows, route_cols, capacity, half)
            total = None
            for k, pick in enumerate(chosen):
                factor = gates[:, k : k + 1].astype(f32) / gate_unit
                scaled = (factor * cotangent[:, k, :].astype(f32)).astype(bf16)
                term = jnp.dot(pick, scaled, preferred_element_type=f32)
                total = term if total is None else total + term
            out[...] = total.astype(bf16)
        pick = sum(chosen[1:], chosen[0])
        outs[2][...] = pick
        store_blocks(
            outs[3:], 0, jnp.dot(pick, tokens[...], preferred_element_type=f32).astype(bf16)
        )

    operands = (routes.T, routes, gates, cotangent, tokens)
    shapes = [(slots, hidden)] * 2 + [(slots, count)] + [(slots // blocks, width)] * blocks
    return run(
        body,
        info,
        (1,),
        [whole(operand.shape) for operand in operands],
        [whole(shape) for shape in shapes],
        [jax.ShapeDtypeStruct(shape, bf16) for shape in shapes],
        *operands,
    )


def pick_far(info, routes, tokens, far_grads, near_grads, capacity, half):
    count, width = tokens.shape
    hidden = far_grads.shape[1]
    slots = half * capacity
    blocks = half if capacity % 16 == 0 else 1

    def body(info, route_rows, route_cols, tokens, far_grads, near_grads, pick_out, *outs):
        chosen = chosen_by(info, info[1], route_rows, route_cols, capacity, half)
        pick = sum(chosen[1:], chosen[0])
        pick_out[...] = pick
        store_blocks(outs, 0, jnp.dot(pick, tokens[...], preferred_element_type=f32).astype(bf16))
        store_blocks(outs, width, far_grads[...])
        store_blocks(outs, width + hidden, near_grads[...])

    operands = (routes.T, routes, tokens, far_grads, near_grads)
    shapes = [(slots, count)] + [(slots // blocks, width + 2 * hidden)] * blocks
    return run(
        body,
        info,
        (1,),
        [whole(operand.shape) for operand in operands],
        [whole(shape) for shape in shapes],
        [jax.ShapeDtypeStruct(shape, bf16) for shape in shapes],
        *operands,
    )


def join(place, far, near):
    blocks = far + near
    width = near[0].shape[1]
    hidden = (far[0].shape[1] - width) // 2
    count = sum(block.shape[0] for block in blocks)

    def body(place, *refs):
        rows, grads = refs[len(blocks) :]
        first = 0
        for number, block in enumerate(refs[: len(blocks)]):
            held = pl.ds(first, block.shape[0])
            start = width if number < len(far) else width + hidden
            rows[held, :] = block[:, :width]
            grads[held, :] = refs[number % len(far)][:, start : start + hidden]
            first += block.shape[0]

    return run(
        body,
        place,
        (1,),
        [whole(block.shape) for block in blocks],
        [whole((count, width)), whole((count, hidden))],
        [
            jax.ShapeDtypeStruct((count, width), bf16),
            jax.ShapeDtypeStruct((count, hidden), bf16),
        ],
        *blocks,
    )


def forward_gate(place, rows, grads, gate):
    pieces, hidden = len(gate), gate[0].shape[0]
    count, width = rows.shape
    tile = tile_of(hidden)

    def body(place, rows, grads, *refs):
        grad_up, factor = refs[pieces:]
        pre_gate = project(place, rows, refs[:pieces])
        sigmoid_gate = jax.nn.sigmoid(pre_gate)
        upstream = grads[...].astype(f32) * sigmoid_gate
        grad_up[...] = (upstream * pre_gate).astype(bf16)
        factor[...] = upstream * (1.0 + pre_gate * (1.0 - sigmoid_gate))

    part = pl.BlockSpec((count, tile), lambda i, _: (0, i))
    return run(
        body,
        place,
        (hidden // tile,),
        [whole((count, width)), part]
        + [pl.BlockSpec((tile, width // pieces), lambda i, _: (i, 0))] * pieces,
        [part, part],
        [
            jax.ShapeDtypeStruct((count, hidden), bf16),
            jax.ShapeDtypeStruct((count, hidden), f32),
        ],
        rows,
        grads,
        *gate,
    )


def forward_up(place, rows, factor, up):
    pieces, hidden = len(up), up[0].shape[0]
    count, width = rows.shape
    tile = tile_of(hidden)

    def body(place, rows, factor, *refs):
        refs[-1][...] = (factor[...] * project(place, rows, refs[:-1])).astype(bf16)

    part = pl.BlockSpec((count, tile), lambda i, _: (0, i))
    return run(
        body,
        place,
        (hidden // tile,),
        [whole((count, width)), part]
        + [pl.BlockSpec((tile, width // pieces), lambda i, _: (i, 0))] * pieces,
        part,
        jax.ShapeDtypeStruct((count, hidden), bf16),
        rows,
        factor,
        *up,
    )


def weight_grads(place, grads, rows, pieces):
    count, hidden = grads.shape
    width = rows.shape[1] // pieces
    tile = tile_of(hidden)

    def body(place, grads, rows, *outs):
        for k, out in enumerate(outs):
            out[...] = lax.dot_general(
                grads[...],
                rows[:, columns(place, k, width)],
                (((0,), (0,)), ((), ())),
                preferred_element_type=f32,
            ).astype(bf16)

    return run(
        body,
        place,
        (hidden // tile,),
        [pl.BlockSpec((count, tile), lambda i, _: (0, i)), whole(rows.shape)],
        [pl.BlockSpec((tile, width), lambda i, _: (i, 0))] * pieces,
        [jax.ShapeDtypeStruct((hidden, width), bf16)] * pieces,
        grads,
        rows,
    )


def input_grads(place, grad_gate, grad_up, gate, up, block_rows):
    count, hidden = grad_gate.shape
    pieces, width = len(gate), gate[0].shape[1]
    tile = tile_of(width)
    blocks = count // block_rows

    def body(place, grad_gate, grad_up, *refs):
        start = pl.program_id(0) * tile
        for k in range(pieces):
            total = jnp.dot(grad_gate[...], refs[k][...], preferred_element_type=f32)
            total += jnp.dot(grad_up[...], refs[pieces + k][...], preferred_element_type=f32)
            total = total.astype(bf16)
            for b, out in enumerate(refs[2 * pieces :]):
                out[:, columns(place, k, width, start, tile)] = total[
                    b * block_rows : (b + 1) * block_rows
                ]

    return run(
        body,
        place,
        (width // tile,),
        [whole((count, hidden))] * 2
        + [pl.BlockSpec((hidden, tile), lambda i, _: (0, i))] * (2 * pieces),
        [whole((block_rows, width * pieces))] * blocks,
        [jax.ShapeDtypeStruct((block_rows, width * pieces), bf16)] * blocks,
        grad_gate,
        grad_up,
        *gate,
        *up,
    )


def adam(index, parts, old, first, second, *results):
    rows, width = old.shape
    sources, _, part, _ = first.shape
    flat = pl.BlockSpec((part, width), lambda i: (i, 0))
    moment = pl.BlockSpec((1, 1, part, width), lambda i: (i, index, 0, 0))
    out = pl.BlockSpec((1, 1, part, width), lambda i: (index, 0, i, 0))
    shape = jax.ShapeDtypeStruct((2, 1, rows, width), old.dtype)
    count = len(parts)

    def body(*refs):
        old_ref, first_ref, second_ref = refs[count : count + 3]
        weights_out, first_out, second_out = refs[-3:]
        gradient = refs[0][...].astype(f32)
        for ref in refs[1:count]:
            gradient += ref[...].astype(f32)
        gradient = gradient / loss_scale
        moment_one = beta_one * first_ref[0, 0].astype(f32) + (1.0 - beta_one) * gradient
        moment_two = (
            beta_two * second_ref[0, 0].astype(f32) + (1.0 - beta_two) * gradient * gradient
        )
        updated = old_ref[...].astype(f32) - step_size * moment_one / (
            jnp.sqrt(moment_two) + adam_eps
        )
        weights_out[0, 0] = updated.astype(bf16)
        first_out[0, 0] = moment_one.astype(bf16)
        second_out[0, 0] = moment_two.astype(bf16)

    return pl.pallas_call(
        body,
        grid=(sources,),
        in_specs=[flat] * (count + 1)
        + [moment] * 2
        + [pl.BlockSpec(memory_space=pl.ANY)] * len(results),
        out_specs=[out] * 3,
        out_shape=[shape] * 3,
        input_output_aliases={count + 3 + i: i for i in range(len(results))},
        compiler_params=pltpu.CompilerParams(vmem_limit_bytes=vmem_bytes),
    )(*parts, old, first, second, *results)


def per_device(
    tokens, routes, router_gates, hidden_cotangent, weights, first_moment, second_moment
):
    row_count, model_width = tokens.shape
    per_token = routes.shape[1]
    hidden_units = hidden_cotangent.shape[2]
    experts = weights.shape[1]
    pieces = model_width // weights.shape[3]
    capacity = 3 * row_count * per_token // (2 * experts)
    half = experts // 2
    mine = lax.axis_index("expert")
    side = mine // half
    info = jnp.stack([mine % half, side]).astype(jnp.int32)
    place = lax.axis_index("dp").astype(jnp.int32).reshape(1)
    swap = [(i, (i + half) % experts) for i in range(experts)]

    def shift(value, step):
        if step % half == 0:
            return value
        pairs = [(i, i // half * half + (i + step) % half) for i in range(experts)]
        return lax.ppermute(value, "expert", pairs)

    def across(value, k):
        return lax.ppermute(value, "dp", [(i, i ^ k) for i in range(pieces)])

    def to_owners(by_owner, *earlier):
        by_owner = after(by_owner, *earlier)
        return lax.all_to_all(by_owner, "expert", split_axis=0, concat_axis=0, tiled=True)

    def along_x(part):
        return [across(part, k) for k in range(2, pieces, 2)]

    def both_cores(parts):
        return [piece for one in parts for piece in (one, across(one, 1))]

    def core_sums(totals):
        sums = []
        for k in range(2, pieces, 2):
            pair = totals[k].astype(f32) + across(totals[k + 1], 1).astype(f32)
            sums.append(pair.astype(bf16))
        return sums

    def scatter(totals, sums):
        sums = [across(pair, 2 * (k + 1)) for k, pair in enumerate(sums)]
        return [totals[0], across(totals[1], 1)] + sums

    other_tokens = lax.ppermute(tokens, "expert", swap)
    other_routes = lax.ppermute(routes, "expert", swap)

    grads_away, near_grads, near_pick, *near_rows = pick_near(
        info, routes, router_gates, hidden_cotangent, tokens, capacity, half
    )
    far_grads = lax.ppermute(grads_away, "expert", swap)

    def send(blocks, direction=1):
        if len(blocks) == 1:
            blocks = [blocks[0][s * capacity : (s + 1) * capacity] for s in range(half)]
        return [shift(block, direction * s) for s, block in enumerate(blocks)]

    def unsplit(blocks):
        return blocks if capacity % 16 == 0 else [jnp.concatenate(blocks, axis=0)]

    near_rows = send(near_rows)
    other_tokens = after(other_tokens, other_routes, far_grads, *near_rows[1:])
    owned = to_owners(jnp.swapaxes(weights, 0, 1), other_tokens)
    other_pick, *far_rows = pick_far(
        info, other_routes, other_tokens, far_grads, near_grads, capacity, half
    )
    far_rows = send(far_rows)
    owned = after(owned, *far_rows[1:])
    owned_gate = owned[:, 0].reshape(hidden_units, -1)
    owned_up = owned[:, 1].reshape(hidden_units, -1)
    owned_first = to_owners(jnp.swapaxes(first_moment, 0, 1), owned)

    gate_x = along_x(owned_gate)
    up_x = along_x(after(owned_up, *gate_x))
    rows, grads = join(place, unsplit(far_rows), unsplit(near_rows))
    gate = both_cores([owned_gate] + [after(piece, rows) for piece in gate_x])
    up = both_cores([owned_up] + up_x)
    grad_up, factor = forward_gate(place, rows, grads, gate)
    up_totals = weight_grads(place, grad_up, rows, pieces)
    up_sums = core_sums(up_totals)
    up_terms = scatter(up_totals, up_sums)
    grad_gate = forward_up(place, rows, after(factor, owned_first, *up_sums), up)
    block_rows = capacity if capacity % 16 == 0 else half * capacity
    back = input_grads(place, grad_gate, grad_up, gate, up, block_rows)
    far_back = send(back[: len(back) // 2], -1)
    near_back = [after(block, *far_back[1:]) for block in back[len(back) // 2 :]]
    near_back = send(near_back, -1)
    owned_second = to_owners(jnp.swapaxes(second_moment, 0, 1), owned_first, up_totals[0])
    gate_totals = weight_grads(place, after(grad_gate, *back), rows, pieces)
    gate_sums = [after(pair, *up_terms) for pair in core_sums(gate_totals)]
    gate_terms = scatter(gate_totals, gate_sums)

    def combine(picker, parts):
        parts = jnp.concatenate(parts, axis=0)
        return jnp.einsum("st,sd->td", picker, parts, preferred_element_type=f32)

    far_sum = after(combine(other_pick, far_back).astype(bf16), owned_second)
    far_sum = lax.ppermute(far_sum, "expert", swap)
    results = adam(1, up_terms, owned_up, owned_first, owned_second)
    results = adam(0, gate_terms, owned_gate, owned_first, owned_second, *results)
    near_back[1:] = [after(block, *results) for block in near_back[1:]]
    near_sum = combine(near_pick, near_back)
    token_grads = (near_sum + far_sum.astype(f32)).astype(bf16)
    return (token_grads, *results)


def solution(mesh):
    placed = (
        P(("dp", "expert"), None),
        P(("dp", "expert"), None),
        P(("dp", "expert"), None),
        P(("dp", "expert"), None, None),
        P(None, None, "expert", "dp"),
        P(None, None, "expert", "dp"),
        P(None, None, "expert", "dp"),
    )
    return jax.shard_map(
        per_device,
        mesh=mesh,
        in_specs=placed,
        out_specs=(
            P(("dp", "expert"), None),
            P(None, "expert", None, "dp"),
            P(None, "expert", None, "dp"),
            P(None, "expert", None, "dp"),
        ),
        check_vma=False,
    )
```

```python
import jax
import jax.numpy as jnp
from jax import lax
from jax.experimental import pallas as pl
from jax.experimental.pallas import tpu as pltpu
from jax.sharding import PartitionSpec as P

gate_unit = 32768.0
loss_scale = 16.0
beta_one = 0.9
beta_two = 0.95
step_size = 0.001
adam_eps = 1e-08
bf16 = jnp.bfloat16
f32 = jnp.float32
vmem_bytes = 32 * 1024 * 1024


def after(value, *others):
    return lax.optimization_barrier((value, *others))[0]


def tile_of(extent):
    return 256 if extent % 256 == 0 else extent


def whole(shape):
    return pl.BlockSpec(shape, lambda *_: (0,) * len(shape))


def run(body, place, grid, in_specs, out_specs, out_shape, *operands):
    return pl.pallas_call(
        body,
        grid_spec=pltpu.PrefetchScalarGridSpec(
            num_scalar_prefetch=1, grid=grid, in_specs=in_specs, out_specs=out_specs
        ),
        out_shape=out_shape,
        compiler_params=pltpu.CompilerParams(vmem_limit_bytes=vmem_bytes),
    )(place, *operands)


def columns(place, k, width, start=0, size=None):
    first = pl.multiple_of((place[0] ^ k) * width + start, 128)
    return pl.ds(first, width if size is None else size)


def project(place, rows, weights):
    total = None
    for k, piece in enumerate(weights):
        term = lax.dot_general(
            rows[:, columns(place, k, piece.shape[1])],
            piece[...],
            (((1,), (1,)), ((), ())),
            preferred_element_type=f32,
        )
        total = term if total is None else total + term
    return total


def chosen_by(info, which, route_rows, route_cols, capacity, half):
    choices, count = route_rows.shape
    slot = lax.broadcasted_iota(jnp.int32, (half * capacity, 1), 0)
    number = jnp.zeros_like(slot)
    for k in range(1, half):
        number += (slot >= k * capacity).astype(jnp.int32)
    expert = info[0] + number
    expert = jnp.where(expert >= half, expert - half, expert) + which * half
    slot = (expert * capacity + slot - number * capacity).astype(f32)
    before = lax.broadcasted_iota(jnp.int32, (count, count), 0)
    before = before < lax.broadcasted_iota(jnp.int32, (count, count), 1)
    chosen = []
    for k in range(choices):
        row = route_rows[k : k + 1, :]
        position = jnp.zeros((1, count), f32)
        for other in range(k + 1):
            same = route_cols[:, other : other + 1] == row
            if other == k:
                same = same & before
            position += jnp.sum(jnp.where(same, 1.0, 0.0), axis=0, keepdims=True)
        target = row.astype(f32) * capacity + position
        chosen.append(jnp.where(target == slot, 1.0, 0.0).astype(bf16))
    return chosen


def store_blocks(refs, start, picked):
    part = picked.shape[0] // len(refs)
    for number, ref in enumerate(refs):
        ref[:, start : start + picked.shape[1]] = picked[number * part : (number + 1) * part]


def pick_near(info, routes, gates, cotangent, tokens, capacity, half):
    count, width = tokens.shape
    hidden = cotangent.shape[2]
    slots = half * capacity
    extra = 16
    blocks = half if capacity % 16 == 0 else 1

    def body(info, route_rows, route_cols, gates, cotangent, tokens, *outs):
        for which, out in ((1 - info[1], outs[0]), (info[1], outs[1])):
            chosen = chosen_by(info, which, route_rows, route_cols, capacity, half)
            total = None
            for k, pick in enumerate(chosen):
                factor = gates[:, k : k + 1].astype(f32) / gate_unit
                scaled = (factor * cotangent[:, k, :].astype(f32)).astype(bf16)
                term = jnp.dot(pick, scaled, preferred_element_type=f32)
                total = term if total is None else total + term
            out[:slots, :] = total.astype(bf16)
        below = jnp.zeros((extra - routes.shape[1], count), f32)
        numbers = jnp.concatenate([route_rows[...].astype(f32), below], axis=0)
        beside = jnp.zeros((extra, hidden - count), f32)
        outs[0][slots:, :] = jnp.concatenate([numbers, beside], axis=1).astype(bf16)
        pick = sum(chosen[1:], chosen[0])
        outs[2][...] = pick
        store_blocks(
            outs[3:], 0, jnp.dot(pick, tokens[...], preferred_element_type=f32).astype(bf16)
        )

    operands = (routes.T, routes, gates, cotangent, tokens)
    shapes = [(slots + extra, hidden), (slots, hidden), (slots, count)]
    shapes += [(slots // blocks, width)] * blocks
    return run(
        body,
        info,
        (1,),
        [whole(operand.shape) for operand in operands],
        [whole(shape) for shape in shapes],
        [jax.ShapeDtypeStruct(shape, bf16) for shape in shapes],
        *operands,
    )


def pick_far(info, routes, tokens, capacity, half):
    count, width = tokens.shape
    slots = half * capacity
    blocks = half if capacity % 16 == 0 else 1

    def body(info, route_rows, route_cols, tokens, pick_out, *outs):
        chosen = chosen_by(info, info[1], route_rows, route_cols, capacity, half)
        pick = sum(chosen[1:], chosen[0])
        pick_out[...] = pick
        store_blocks(outs, 0, jnp.dot(pick, tokens[...], preferred_element_type=f32).astype(bf16))

    operands = (routes.T, routes, tokens)
    shapes = [(slots, count)] + [(slots // blocks, width)] * blocks
    return run(
        body,
        info,
        (1,),
        [whole(operand.shape) for operand in operands],
        [whole(shape) for shape in shapes],
        [jax.ShapeDtypeStruct(shape, bf16) for shape in shapes],
        *operands,
    )


def join(place, blocks):
    width = blocks[0].shape[1]
    count = sum(block.shape[0] for block in blocks)

    def body(place, *refs):
        first = 0
        for block in refs[:-1]:
            refs[-1][first : first + block.shape[0], :] = block[...]
            first += block.shape[0]

    return run(
        body,
        place,
        (1,),
        [whole(block.shape) for block in blocks],
        whole((count, width)),
        jax.ShapeDtypeStruct((count, width), bf16),
        *blocks,
    )


def forward_gate(place, rows, grads, gate):
    pieces, hidden = len(gate), gate[0].shape[0]
    count, width = rows.shape
    tile = tile_of(hidden)

    def body(place, rows, grads, *refs):
        grad_up, factor = refs[pieces:]
        pre_gate = project(place, rows, refs[:pieces])
        sigmoid_gate = jax.nn.sigmoid(pre_gate)
        upstream = grads[...].astype(f32) * sigmoid_gate
        grad_up[...] = (upstream * pre_gate).astype(bf16)
        factor[...] = upstream * (1.0 + pre_gate * (1.0 - sigmoid_gate))

    part = pl.BlockSpec((count, tile), lambda i, _: (0, i))
    return run(
        body,
        place,
        (hidden // tile,),
        [whole((count, width)), part]
        + [pl.BlockSpec((tile, width // pieces), lambda i, _: (i, 0))] * pieces,
        [part, part],
        [
            jax.ShapeDtypeStruct((count, hidden), bf16),
            jax.ShapeDtypeStruct((count, hidden), f32),
        ],
        rows,
        grads,
        *gate,
    )


def forward_up(place, rows, factor, up):
    pieces, hidden = len(up), up[0].shape[0]
    count, width = rows.shape
    tile = tile_of(hidden)

    def body(place, rows, factor, *refs):
        refs[-1][...] = (factor[...] * project(place, rows, refs[:-1])).astype(bf16)

    part = pl.BlockSpec((count, tile), lambda i, _: (0, i))
    return run(
        body,
        place,
        (hidden // tile,),
        [whole((count, width)), part]
        + [pl.BlockSpec((tile, width // pieces), lambda i, _: (i, 0))] * pieces,
        part,
        jax.ShapeDtypeStruct((count, hidden), bf16),
        rows,
        factor,
        *up,
    )


def weight_grads(place, grads, rows, pieces):
    count, hidden = grads.shape
    width = rows.shape[1] // pieces
    tile = tile_of(hidden)

    def body(place, grads, rows, *outs):
        for k, out in enumerate(outs):
            out[...] = lax.dot_general(
                grads[...],
                rows[:, columns(place, k, width)],
                (((0,), (0,)), ((), ())),
                preferred_element_type=f32,
            ).astype(bf16)

    return run(
        body,
        place,
        (hidden // tile,),
        [pl.BlockSpec((count, tile), lambda i, _: (0, i)), whole(rows.shape)],
        [pl.BlockSpec((tile, width), lambda i, _: (i, 0))] * pieces,
        [jax.ShapeDtypeStruct((hidden, width), bf16)] * pieces,
        grads,
        rows,
    )


def input_grads(place, grad_gate, grad_up, gate, up, block_rows):
    count, hidden = grad_gate.shape
    pieces, width = len(gate), gate[0].shape[1]
    tile = tile_of(width)
    blocks = count // block_rows

    def body(place, grad_gate, grad_up, *refs):
        start = pl.program_id(0) * tile
        for k in range(pieces):
            total = jnp.dot(grad_gate[...], refs[k][...], preferred_element_type=f32)
            total += jnp.dot(grad_up[...], refs[pieces + k][...], preferred_element_type=f32)
            total = total.astype(bf16)
            for b, out in enumerate(refs[2 * pieces :]):
                out[:, columns(place, k, width, start, tile)] = total[
                    b * block_rows : (b + 1) * block_rows
                ]

    return run(
        body,
        place,
        (width // tile,),
        [whole((count, hidden))] * 2
        + [pl.BlockSpec((hidden, tile), lambda i, _: (0, i))] * (2 * pieces),
        [whole((block_rows, width * pieces))] * blocks,
        [jax.ShapeDtypeStruct((block_rows, width * pieces), bf16)] * blocks,
        grad_gate,
        grad_up,
        *gate,
        *up,
    )


def adam(index, parts, old, first, second, *results):
    rows, width = old.shape
    sources, _, part, _ = first.shape
    flat = pl.BlockSpec((part, width), lambda i: (i, 0))
    moment = pl.BlockSpec((1, 1, part, width), lambda i: (i, index, 0, 0))
    out = pl.BlockSpec((1, 1, part, width), lambda i: (index, 0, i, 0))
    shape = jax.ShapeDtypeStruct((2, 1, rows, width), old.dtype)
    count = len(parts)

    def body(*refs):
        old_ref, first_ref, second_ref = refs[count : count + 3]
        weights_out, first_out, second_out = refs[-3:]
        gradient = refs[0][...].astype(f32)
        for ref in refs[1:count]:
            gradient += ref[...].astype(f32)
        gradient = gradient / loss_scale
        moment_one = beta_one * first_ref[0, 0].astype(f32) + (1.0 - beta_one) * gradient
        moment_two = (
            beta_two * second_ref[0, 0].astype(f32) + (1.0 - beta_two) * gradient * gradient
        )
        updated = old_ref[...].astype(f32) - step_size * moment_one / (
            jnp.sqrt(moment_two) + adam_eps
        )
        weights_out[0, 0] = updated.astype(bf16)
        first_out[0, 0] = moment_one.astype(bf16)
        second_out[0, 0] = moment_two.astype(bf16)

    return pl.pallas_call(
        body,
        grid=(sources,),
        in_specs=[flat] * (count + 1)
        + [moment] * 2
        + [pl.BlockSpec(memory_space=pl.ANY)] * len(results),
        out_specs=[out] * 3,
        out_shape=[shape] * 3,
        input_output_aliases={count + 3 + i: i for i in range(len(results))},
        compiler_params=pltpu.CompilerParams(vmem_limit_bytes=vmem_bytes),
    )(*parts, old, first, second, *results)


def per_device(
    tokens, routes, router_gates, hidden_cotangent, weights, first_moment, second_moment
):
    row_count, model_width = tokens.shape
    per_token = routes.shape[1]
    hidden_units = hidden_cotangent.shape[2]
    experts = weights.shape[1]
    pieces = model_width // weights.shape[3]
    capacity = 3 * row_count * per_token // (2 * experts)
    half = experts // 2
    mine = lax.axis_index("expert")
    side = mine // half
    info = jnp.stack([mine % half, side]).astype(jnp.int32)
    place = lax.axis_index("dp").astype(jnp.int32).reshape(1)
    swap = [(i, (i + half) % experts) for i in range(experts)]

    def shift(value, step):
        if step % half == 0:
            return value
        pairs = [(i, i // half * half + (i + step) % half) for i in range(experts)]
        return lax.ppermute(value, "expert", pairs)

    def across(value, k):
        return lax.ppermute(value, "dp", [(i, i ^ k) for i in range(pieces)])

    def to_owners(by_owner, *earlier):
        by_owner = after(by_owner, *earlier)
        return lax.all_to_all(by_owner, "expert", split_axis=0, concat_axis=0, tiled=True)

    def along_x(part):
        return [across(part, k) for k in range(2, pieces, 2)]

    def both_cores(parts):
        return [piece for one in parts for piece in (one, across(one, 1))]

    def core_sums(totals):
        sums = []
        for k in range(2, pieces, 2):
            pair = totals[k].astype(f32) + across(totals[k + 1], 1).astype(f32)
            sums.append(pair.astype(bf16))
        return sums

    def scatter(totals, sums):
        sums = [across(pair, 2 * (k + 1)) for k, pair in enumerate(sums)]
        return [totals[0], across(totals[1], 1)] + sums

    other_tokens = lax.ppermute(tokens, "expert", swap)

    grads_away, near_grads, near_pick, *near_rows = pick_near(
        info, routes, router_gates, hidden_cotangent, tokens, capacity, half
    )
    arrived = lax.ppermute(grads_away, "expert", swap)
    far_grads = arrived[: half * capacity]
    other_routes = arrived[half * capacity : half * capacity + per_token, :row_count]
    other_routes = other_routes.astype(jnp.int32).T

    def send(blocks, direction=1):
        if len(blocks) == 1:
            blocks = [blocks[0][s * capacity : (s + 1) * capacity] for s in range(half)]
        return [shift(block, direction * s) for s, block in enumerate(blocks)]

    def unsplit(blocks):
        return blocks if capacity % 16 == 0 else [jnp.concatenate(blocks, axis=0)]

    near_rows = send(near_rows)
    other_tokens = after(other_tokens, arrived, *near_rows[1:])
    owned = to_owners(jnp.swapaxes(weights, 0, 1), other_tokens)
    other_pick, *far_rows = pick_far(info, other_routes, other_tokens, capacity, half)
    far_rows = send(far_rows)
    pairs = [part.reshape(half, capacity, hidden_units) for part in (far_grads, near_grads)]
    pairs = jnp.concatenate(pairs, axis=1)
    pairs = [shift(after(pairs[s], other_tokens), s) for s in range(half)]
    owned = after(owned, *far_rows[1:], *pairs[1:])
    owned_gate = owned[:, 0].reshape(hidden_units, -1)
    owned_up = owned[:, 1].reshape(hidden_units, -1)
    owned_first = to_owners(jnp.swapaxes(first_moment, 0, 1), owned)

    gate_x = along_x(owned_gate)
    up_x = along_x(after(owned_up, *gate_x))
    rows = join(place, unsplit(far_rows) + unsplit(near_rows))
    grads = jnp.stack(pairs).reshape(half, 2, capacity, hidden_units)
    grads = jnp.swapaxes(grads, 0, 1).reshape(2 * half * capacity, hidden_units)
    gate = both_cores([owned_gate] + [after(piece, rows) for piece in gate_x])
    up = both_cores([owned_up] + up_x)
    grad_up, factor = forward_gate(place, rows, grads, gate)
    up_totals = weight_grads(place, grad_up, rows, pieces)
    up_sums = core_sums(up_totals)
    up_terms = scatter(up_totals, up_sums)
    grad_gate = forward_up(place, rows, after(factor, owned_first, *up_sums), up)
    block_rows = capacity if capacity % 16 == 0 else half * capacity
    back = input_grads(place, grad_gate, grad_up, gate, up, block_rows)
    far_back = send(back[: len(back) // 2], -1)
    near_back = [after(block, *far_back[1:]) for block in back[len(back) // 2 :]]
    near_back = send(near_back, -1)
    owned_second = to_owners(jnp.swapaxes(second_moment, 0, 1), owned_first, up_totals[0])
    gate_totals = weight_grads(place, after(grad_gate, *back), rows, pieces)
    gate_sums = [after(pair, *up_terms) for pair in core_sums(gate_totals)]
    gate_terms = scatter(gate_totals, gate_sums)

    def combine(picker, parts):
        parts = jnp.concatenate(parts, axis=0)
        return jnp.einsum("st,sd->td", picker, parts, preferred_element_type=f32)

    far_sum = after(combine(other_pick, far_back).astype(bf16), owned_second)
    far_sum = lax.ppermute(far_sum, "expert", swap)
    results = adam(1, up_terms, owned_up, owned_first, owned_second)
    results = adam(0, gate_terms, owned_gate, owned_first, owned_second, *results)
    near_back[1:] = [after(block, *results) for block in near_back[1:]]
    near_sum = combine(near_pick, near_back)
    token_grads = (near_sum + far_sum.astype(f32)).astype(bf16)
    return (token_grads, *results)


def solution(mesh):
    placed = (
        P(("dp", "expert"), None),
        P(("dp", "expert"), None),
        P(("dp", "expert"), None),
        P(("dp", "expert"), None, None),
        P(None, None, "expert", "dp"),
        P(None, None, "expert", "dp"),
        P(None, None, "expert", "dp"),
    )
    return jax.shard_map(
        per_device,
        mesh=mesh,
        in_specs=placed,
        out_specs=(
            P(("dp", "expert"), None),
            P(None, "expert", None, "dp"),
            P(None, "expert", None, "dp"),
            P(None, "expert", None, "dp"),
        ),
        check_vma=False,
    )
```

```python
import jax
import jax.numpy as jnp
from jax import lax
from jax.experimental import pallas as pl
from jax.experimental.pallas import tpu as pltpu
from jax.sharding import PartitionSpec as P

gate_unit = 32768.0
loss_scale = 16.0
beta_one = 0.9
beta_two = 0.95
step_size = 0.001
adam_eps = 1e-08
bf16 = jnp.bfloat16
f32 = jnp.float32
vmem_bytes = 32 * 1024 * 1024


def after(value, *others):
    return lax.optimization_barrier((value, *others))[0]


def tile_of(extent):
    return 256 if extent % 256 == 0 else extent


def whole(shape):
    return pl.BlockSpec(shape, lambda *_: (0,) * len(shape))


def run(body, place, grid, in_specs, out_specs, out_shape, *operands):
    return pl.pallas_call(
        body,
        grid_spec=pltpu.PrefetchScalarGridSpec(
            num_scalar_prefetch=1, grid=grid, in_specs=in_specs, out_specs=out_specs
        ),
        out_shape=out_shape,
        compiler_params=pltpu.CompilerParams(vmem_limit_bytes=vmem_bytes),
    )(place, *operands)


def columns(place, k, width, start=0, size=None):
    first = pl.multiple_of((place[0] ^ k) * width + start, 128)
    return pl.ds(first, width if size is None else size)


def project(place, rows, weights):
    total = None
    for k, piece in enumerate(weights):
        term = lax.dot_general(
            rows[:, columns(place, k, piece.shape[1])],
            piece[...],
            (((1,), (1,)), ((), ())),
            preferred_element_type=f32,
        )
        total = term if total is None else total + term
    return total


def chosen_by(info, which, route_rows, route_cols, capacity, half):
    choices, count = route_rows.shape
    slot = lax.broadcasted_iota(jnp.int32, (half * capacity, 1), 0)
    number = jnp.zeros_like(slot)
    for k in range(1, half):
        number += (slot >= k * capacity).astype(jnp.int32)
    expert = info[0] + number
    expert = jnp.where(expert >= half, expert - half, expert) + which * half
    slot = (expert * capacity + slot - number * capacity).astype(f32)
    before = lax.broadcasted_iota(jnp.int32, (count, count), 0)
    before = before < lax.broadcasted_iota(jnp.int32, (count, count), 1)
    chosen = []
    for k in range(choices):
        row = route_rows[k : k + 1, :]
        position = jnp.zeros((1, count), f32)
        for other in range(k + 1):
            same = route_cols[:, other : other + 1] == row
            if other == k:
                same = same & before
            position += jnp.sum(jnp.where(same, 1.0, 0.0), axis=0, keepdims=True)
        target = row.astype(f32) * capacity + position
        chosen.append(jnp.where(target == slot, 1.0, 0.0).astype(bf16))
    return chosen


def store_blocks(refs, start, picked):
    part = picked.shape[0] // len(refs)
    for number, ref in enumerate(refs):
        ref[:, start : start + picked.shape[1]] = picked[number * part : (number + 1) * part]


def pick_near(info, routes, gates, cotangent, tokens, capacity, half):
    count, width = tokens.shape
    hidden = cotangent.shape[2]
    slots = half * capacity
    extra = 16
    blocks = half if capacity % 16 == 0 else 1

    def body(info, route_rows, route_cols, gates, cotangent, tokens, *outs):
        for which, out in ((1 - info[1], outs[0]), (info[1], outs[1])):
            chosen = chosen_by(info, which, route_rows, route_cols, capacity, half)
            total = None
            for k, pick in enumerate(chosen):
                factor = gates[:, k : k + 1].astype(f32) / gate_unit
                scaled = (factor * cotangent[:, k, :].astype(f32)).astype(bf16)
                term = jnp.dot(pick, scaled, preferred_element_type=f32)
                total = term if total is None else total + term
            out[:slots, :] = total.astype(bf16)
        below = jnp.zeros((extra - routes.shape[1], count), f32)
        numbers = jnp.concatenate([route_rows[...].astype(f32), below], axis=0)
        beside = jnp.zeros((extra, hidden - count), f32)
        outs[0][slots:, :] = jnp.concatenate([numbers, beside], axis=1).astype(bf16)
        pick = sum(chosen[1:], chosen[0])
        outs[2][...] = pick
        store_blocks(
            outs[3:], 0, jnp.dot(pick, tokens[...], preferred_element_type=f32).astype(bf16)
        )

    operands = (routes.T, routes, gates, cotangent, tokens)
    shapes = [(slots + extra, hidden), (slots, hidden), (slots, count)]
    shapes += [(slots // blocks, width)] * blocks
    return run(
        body,
        info,
        (1,),
        [whole(operand.shape) for operand in operands],
        [whole(shape) for shape in shapes],
        [jax.ShapeDtypeStruct(shape, bf16) for shape in shapes],
        *operands,
    )


def pick_far(info, routes, tokens, capacity, half):
    count, width = tokens.shape
    slots = half * capacity
    blocks = half if capacity % 16 == 0 else 1

    def body(info, route_rows, route_cols, tokens, pick_out, *outs):
        chosen = chosen_by(info, info[1], route_rows, route_cols, capacity, half)
        pick = sum(chosen[1:], chosen[0])
        pick_out[...] = pick
        store_blocks(outs, 0, jnp.dot(pick, tokens[...], preferred_element_type=f32).astype(bf16))

    operands = (routes.T, routes, tokens)
    shapes = [(slots, count)] + [(slots // blocks, width)] * blocks
    return run(
        body,
        info,
        (1,),
        [whole(operand.shape) for operand in operands],
        [whole(shape) for shape in shapes],
        [jax.ShapeDtypeStruct(shape, bf16) for shape in shapes],
        *operands,
    )


def join(place, blocks):
    width = blocks[0].shape[1]
    count = sum(block.shape[0] for block in blocks)

    def body(place, *refs):
        first = 0
        for block in refs[:-1]:
            refs[-1][first : first + block.shape[0], :] = block[...]
            first += block.shape[0]

    return run(
        body,
        place,
        (1,),
        [whole(block.shape) for block in blocks],
        whole((count, width)),
        jax.ShapeDtypeStruct((count, width), bf16),
        *blocks,
    )


def forward_gate(place, rows, grads, gate):
    pieces, hidden = len(gate), gate[0].shape[0]
    count, width = rows.shape
    tile = tile_of(hidden)

    def body(place, rows, grads, *refs):
        grad_up, factor = refs[pieces:]
        pre_gate = project(place, rows, refs[:pieces])
        sigmoid_gate = jax.nn.sigmoid(pre_gate)
        upstream = grads[...].astype(f32) * sigmoid_gate
        grad_up[...] = (upstream * pre_gate).astype(bf16)
        factor[...] = upstream * (1.0 + pre_gate * (1.0 - sigmoid_gate))

    part = pl.BlockSpec((count, tile), lambda i, _: (0, i))
    return run(
        body,
        place,
        (hidden // tile,),
        [whole((count, width)), part]
        + [pl.BlockSpec((tile, width // pieces), lambda i, _: (i, 0))] * pieces,
        [part, part],
        [
            jax.ShapeDtypeStruct((count, hidden), bf16),
            jax.ShapeDtypeStruct((count, hidden), f32),
        ],
        rows,
        grads,
        *gate,
    )


def forward_up(place, rows, factor, up):
    pieces, hidden = len(up), up[0].shape[0]
    count, width = rows.shape
    tile = tile_of(hidden)

    def body(place, rows, factor, *refs):
        refs[-1][...] = (factor[...] * project(place, rows, refs[:-1])).astype(bf16)

    part = pl.BlockSpec((count, tile), lambda i, _: (0, i))
    return run(
        body,
        place,
        (hidden // tile,),
        [whole((count, width)), part]
        + [pl.BlockSpec((tile, width // pieces), lambda i, _: (i, 0))] * pieces,
        part,
        jax.ShapeDtypeStruct((count, hidden), bf16),
        rows,
        factor,
        *up,
    )


def weight_grads(place, grads, rows, pieces):
    count, hidden = grads.shape
    width = rows.shape[1] // pieces
    tile = tile_of(hidden)

    def body(place, grads, rows, *outs):
        for k, out in enumerate(outs):
            out[...] = lax.dot_general(
                grads[...],
                rows[:, columns(place, k, width)],
                (((0,), (0,)), ((), ())),
                preferred_element_type=f32,
            ).astype(bf16)

    return run(
        body,
        place,
        (hidden // tile,),
        [pl.BlockSpec((count, tile), lambda i, _: (0, i)), whole(rows.shape)],
        [pl.BlockSpec((tile, width), lambda i, _: (i, 0))] * pieces,
        [jax.ShapeDtypeStruct((hidden, width), bf16)] * pieces,
        grads,
        rows,
    )


def input_grads(place, grad_gate, grad_up, gate, up, block_rows):
    count, hidden = grad_gate.shape
    pieces, width = len(gate), gate[0].shape[1]
    tile = tile_of(width)
    blocks = count // block_rows

    def body(place, grad_gate, grad_up, *refs):
        start = pl.program_id(0) * tile
        for k in range(pieces):
            total = jnp.dot(grad_gate[...], refs[k][...], preferred_element_type=f32)
            total += jnp.dot(grad_up[...], refs[pieces + k][...], preferred_element_type=f32)
            total = total.astype(bf16)
            for b, out in enumerate(refs[2 * pieces :]):
                out[:, columns(place, k, width, start, tile)] = total[
                    b * block_rows : (b + 1) * block_rows
                ]

    return run(
        body,
        place,
        (width // tile,),
        [whole((count, hidden))] * 2
        + [pl.BlockSpec((hidden, tile), lambda i, _: (0, i))] * (2 * pieces),
        [whole((block_rows, width * pieces))] * blocks,
        [jax.ShapeDtypeStruct((block_rows, width * pieces), bf16)] * blocks,
        grad_gate,
        grad_up,
        *gate,
        *up,
    )


def adam(index, parts, old, first, second, *results):
    rows, width = old.shape
    sources, _, part, _ = first.shape
    flat = pl.BlockSpec((part, width), lambda i: (i, 0))
    moment = pl.BlockSpec((1, 1, part, width), lambda i: (i, index, 0, 0))
    out = pl.BlockSpec((1, 1, part, width), lambda i: (index, 0, i, 0))
    shape = jax.ShapeDtypeStruct((2, 1, rows, width), old.dtype)
    count = len(parts)

    def body(*refs):
        old_ref, first_ref, second_ref = refs[count : count + 3]
        weights_out, first_out, second_out = refs[-3:]
        gradient = refs[0][...].astype(f32)
        for ref in refs[1:count]:
            gradient += ref[...].astype(f32)
        gradient = gradient / loss_scale
        moment_one = beta_one * first_ref[0, 0].astype(f32) + (1.0 - beta_one) * gradient
        moment_two = (
            beta_two * second_ref[0, 0].astype(f32) + (1.0 - beta_two) * gradient * gradient
        )
        updated = old_ref[...].astype(f32) - step_size * moment_one / (
            jnp.sqrt(moment_two) + adam_eps
        )
        weights_out[0, 0] = updated.astype(bf16)
        first_out[0, 0] = moment_one.astype(bf16)
        second_out[0, 0] = moment_two.astype(bf16)

    return pl.pallas_call(
        body,
        grid=(sources,),
        in_specs=[flat] * (count + 1)
        + [moment] * 2
        + [pl.BlockSpec(memory_space=pl.ANY)] * len(results),
        out_specs=[out] * 3,
        out_shape=[shape] * 3,
        input_output_aliases={count + 3 + i: i for i in range(len(results))},
        compiler_params=pltpu.CompilerParams(vmem_limit_bytes=vmem_bytes),
    )(*parts, old, first, second, *results)


def per_device(
    tokens, routes, router_gates, hidden_cotangent, weights, first_moment, second_moment
):
    row_count, model_width = tokens.shape
    per_token = routes.shape[1]
    hidden_units = hidden_cotangent.shape[2]
    experts = weights.shape[1]
    pieces = model_width // weights.shape[3]
    capacity = 3 * row_count * per_token // (2 * experts)
    half = experts // 2
    mine = lax.axis_index("expert")
    side = mine // half
    info = jnp.stack([mine % half, side]).astype(jnp.int32)
    place = lax.axis_index("dp").astype(jnp.int32).reshape(1)
    swap = [(i, (i + half) % experts) for i in range(experts)]

    def shift(value, step):
        if step % half == 0:
            return value
        pairs = [(i, i // half * half + (i + step) % half) for i in range(experts)]
        return lax.ppermute(value, "expert", pairs)

    def across(value, k):
        return lax.ppermute(value, "dp", [(i, i ^ k) for i in range(pieces)])

    def to_owners(by_owner, *earlier):
        by_owner = after(by_owner, *earlier)
        return lax.all_to_all(by_owner, "expert", split_axis=0, concat_axis=0, tiled=True)

    def along_x(part):
        return [across(part, k) for k in range(2, pieces, 2)]

    def both_cores(parts):
        return [piece for one in parts for piece in (one, across(one, 1))]

    def core_sums(totals):
        sums = []
        for k in range(2, pieces, 2):
            pair = totals[k].astype(f32) + across(totals[k + 1], 1).astype(f32)
            sums.append(pair.astype(bf16))
        return sums

    def scatter(totals, sums):
        sums = [across(pair, 2 * (k + 1)) for k, pair in enumerate(sums)]
        return [totals[0], across(totals[1], 1)] + sums

    other_tokens = lax.ppermute(tokens, "expert", swap)

    grads_away, near_grads, near_pick, *near_rows = pick_near(
        info, routes, router_gates, hidden_cotangent, tokens, capacity, half
    )
    arrived = lax.ppermute(grads_away, "expert", swap)
    far_grads = arrived[: half * capacity]
    other_routes = arrived[half * capacity : half * capacity + per_token, :row_count]
    other_routes = other_routes.astype(jnp.int32).T

    def send(blocks, direction=1):
        if len(blocks) == 1:
            blocks = [blocks[0][s * capacity : (s + 1) * capacity] for s in range(half)]
        return [shift(block, direction * s) for s, block in enumerate(blocks)]

    def unsplit(blocks):
        return blocks if capacity % 16 == 0 else [jnp.concatenate(blocks, axis=0)]

    near_rows = send(near_rows)
    other_tokens = after(other_tokens, arrived, *near_rows[1:])
    owned = to_owners(jnp.swapaxes(weights, 0, 1), other_tokens)
    other_pick, *far_rows = pick_far(info, other_routes, other_tokens, capacity, half)
    far_rows = send(far_rows)
    owned = after(owned, *far_rows[1:])
    pairs = [part.reshape(half, capacity, hidden_units) for part in (far_grads, near_grads)]
    pairs = jnp.concatenate(pairs, axis=1)
    pairs = [shift(after(pairs[s], owned), s) for s in range(half)]
    owned_gate = owned[:, 0].reshape(hidden_units, -1)
    owned_up = owned[:, 1].reshape(hidden_units, -1)
    owned_first = to_owners(jnp.swapaxes(first_moment, 0, 1), owned)

    gate_x = along_x(owned_gate)
    up_x = along_x(after(owned_up, *gate_x))
    rows = join(place, unsplit(far_rows) + unsplit(near_rows))
    grads = jnp.stack(pairs).reshape(half, 2, capacity, hidden_units)
    grads = jnp.swapaxes(grads, 0, 1).reshape(2 * half * capacity, hidden_units)
    grads = after(grads, *up_x)
    gate = both_cores([owned_gate] + [after(piece, rows) for piece in gate_x])
    up = both_cores([owned_up] + up_x)
    grad_up, factor = forward_gate(place, rows, grads, gate)
    up_totals = weight_grads(place, grad_up, rows, pieces)
    up_sums = core_sums(up_totals)
    up_terms = scatter(up_totals, up_sums)
    grad_gate = forward_up(place, rows, after(factor, owned_first, *up_sums), up)
    block_rows = capacity if capacity % 16 == 0 else half * capacity
    back = input_grads(place, grad_gate, grad_up, gate, up, block_rows)
    far_back = send(back[: len(back) // 2], -1)
    near_back = [after(block, *far_back[1:]) for block in back[len(back) // 2 :]]
    near_back = send(near_back, -1)
    owned_second = to_owners(jnp.swapaxes(second_moment, 0, 1), owned_first, *pairs[1:])
    gate_totals = weight_grads(place, after(grad_gate, *back), rows, pieces)
    gate_sums = [after(pair, *up_terms) for pair in core_sums(gate_totals)]
    gate_terms = scatter(gate_totals, gate_sums)

    def combine(picker, parts):
        parts = jnp.concatenate(parts, axis=0)
        return jnp.einsum("st,sd->td", picker, parts, preferred_element_type=f32)

    far_sum = after(combine(other_pick, far_back).astype(bf16), owned_second)
    far_sum = lax.ppermute(far_sum, "expert", swap)
    results = adam(1, up_terms, owned_up, owned_first, owned_second)
    results = adam(0, gate_terms, owned_gate, owned_first, owned_second, *results)
    near_back[1:] = [after(block, *results) for block in near_back[1:]]
    near_sum = combine(near_pick, near_back)
    token_grads = (near_sum + far_sum.astype(f32)).astype(bf16)
    return (token_grads, *results)


def solution(mesh):
    placed = (
        P(("dp", "expert"), None),
        P(("dp", "expert"), None),
        P(("dp", "expert"), None),
        P(("dp", "expert"), None, None),
        P(None, None, "expert", "dp"),
        P(None, None, "expert", "dp"),
        P(None, None, "expert", "dp"),
    )
    return jax.shard_map(
        per_device,
        mesh=mesh,
        in_specs=placed,
        out_specs=(
            P(("dp", "expert"), None),
            P(None, "expert", None, "dp"),
            P(None, "expert", None, "dp"),
            P(None, "expert", None, "dp"),
        ),
        check_vma=False,
    )
```

```python
import jax
import jax.numpy as jnp
from jax import lax
from jax.experimental import pallas as pl
from jax.experimental.pallas import tpu as pltpu
from jax.sharding import PartitionSpec as P

gate_unit = 32768.0
loss_scale = 16.0
beta_one = 0.9
beta_two = 0.95
step_size = 0.001
adam_eps = 1e-08
bf16 = jnp.bfloat16
f32 = jnp.float32
vmem_bytes = 32 * 1024 * 1024


def after(value, *others):
    return lax.optimization_barrier((value, *others))[0]


def tile_of(extent):
    return 256 if extent % 256 == 0 else extent


def whole(shape):
    return pl.BlockSpec(shape, lambda *_: (0,) * len(shape))


def run(body, place, grid, in_specs, out_specs, out_shape, *operands):
    return pl.pallas_call(
        body,
        grid_spec=pltpu.PrefetchScalarGridSpec(
            num_scalar_prefetch=1, grid=grid, in_specs=in_specs, out_specs=out_specs
        ),
        out_shape=out_shape,
        compiler_params=pltpu.CompilerParams(vmem_limit_bytes=vmem_bytes),
    )(place, *operands)


def columns(place, k, width, start=0, size=None):
    first = pl.multiple_of((place[0] ^ k) * width + start, 128)
    return pl.ds(first, width if size is None else size)


def project(place, rows, weights):
    total = None
    for k, piece in enumerate(weights):
        term = lax.dot_general(
            rows[:, columns(place, k, piece.shape[1])],
            piece[...],
            (((1,), (1,)), ((), ())),
            preferred_element_type=f32,
        )
        total = term if total is None else total + term
    return total


def forward_gate(place, blocks, upstream, gate):
    pieces, hidden = len(gate), gate[0].shape[0]
    width = gate[0].shape[1] * pieces
    count = sum(block.shape[0] for block in blocks)
    tile = tile_of(hidden)

    def body(place, *refs):
        block_refs, refs = refs[: len(blocks)], refs[len(blocks) :]
        up_ref, gate_refs = refs[0], refs[1 : 1 + pieces]
        rows, grad_up, factor = refs[1 + pieces :]

        @pl.when(pl.program_id(0) == 0)
        def _():
            first = 0
            for block in block_refs:
                rows[first : first + block.shape[0], :] = block[...]
                first += block.shape[0]

        pre_gate = project(place, rows, gate_refs)
        sigmoid_gate = jax.nn.sigmoid(pre_gate)
        upstream = up_ref[...].astype(f32) * sigmoid_gate
        grad_up[...] = (upstream * pre_gate).astype(bf16)
        factor[...] = upstream * (1.0 + pre_gate * (1.0 - sigmoid_gate))

    part = pl.BlockSpec((count, tile), lambda i, _: (0, i))
    return run(
        body,
        place,
        (hidden // tile,),
        [whole(block.shape) for block in blocks]
        + [part]
        + [pl.BlockSpec((tile, width // pieces), lambda i, _: (i, 0))] * pieces,
        [whole((count, width)), part, part],
        [
            jax.ShapeDtypeStruct((count, width), bf16),
            jax.ShapeDtypeStruct((count, hidden), bf16),
            jax.ShapeDtypeStruct((count, hidden), f32),
        ],
        *blocks,
        upstream,
        *gate,
    )


def forward_up(place, rows, factor, up):
    pieces, hidden = len(up), up[0].shape[0]
    count, width = rows.shape
    tile = tile_of(hidden)

    def body(place, rows, factor, *refs):
        refs[-1][...] = (factor[...] * project(place, rows, refs[:-1])).astype(bf16)

    part = pl.BlockSpec((count, tile), lambda i, _: (0, i))
    return run(
        body,
        place,
        (hidden // tile,),
        [whole((count, width)), part]
        + [pl.BlockSpec((tile, width // pieces), lambda i, _: (i, 0))] * pieces,
        part,
        jax.ShapeDtypeStruct((count, hidden), bf16),
        rows,
        factor,
        *up,
    )


def weight_grads(place, grads, rows, pieces):
    count, hidden = grads.shape
    width = rows.shape[1] // pieces
    tile = tile_of(hidden)

    def body(place, grads, rows, *outs):
        for k, out in enumerate(outs):
            out[...] = lax.dot_general(
                grads[...],
                rows[:, columns(place, k, width)],
                (((0,), (0,)), ((), ())),
                preferred_element_type=f32,
            ).astype(bf16)

    return run(
        body,
        place,
        (hidden // tile,),
        [pl.BlockSpec((count, tile), lambda i, _: (0, i)), whole(rows.shape)],
        [pl.BlockSpec((tile, width), lambda i, _: (i, 0))] * pieces,
        [jax.ShapeDtypeStruct((hidden, width), bf16)] * pieces,
        grads,
        rows,
    )


def input_grads(place, grad_gate, grad_up, gate, up, block_rows):
    count, hidden = grad_gate.shape
    pieces, width = len(gate), gate[0].shape[1]
    tile = tile_of(width)
    blocks = count // block_rows

    def body(place, grad_gate, grad_up, *refs):
        start = pl.program_id(0) * tile
        for k in range(pieces):
            total = jnp.dot(grad_gate[...], refs[k][...], preferred_element_type=f32)
            total += jnp.dot(grad_up[...], refs[pieces + k][...], preferred_element_type=f32)
            total = total.astype(bf16)
            for b, out in enumerate(refs[2 * pieces :]):
                out[:, columns(place, k, width, start, tile)] = total[
                    b * block_rows : (b + 1) * block_rows
                ]

    return run(
        body,
        place,
        (width // tile,),
        [whole((count, hidden))] * 2
        + [pl.BlockSpec((hidden, tile), lambda i, _: (0, i))] * (2 * pieces),
        [whole((block_rows, width * pieces))] * blocks,
        [jax.ShapeDtypeStruct((block_rows, width * pieces), bf16)] * blocks,
        grad_gate,
        grad_up,
        *gate,
        *up,
    )


def adam(index, parts, old, first_old, second_old, *results):
    rows, width = old.shape
    sources, _, part, _ = second_old.shape
    flat = pl.BlockSpec((part, width), lambda i: (i, 0))
    moment = pl.BlockSpec((1, 1, part, width), lambda i: (i, index, 0, 0))
    out = pl.BlockSpec((1, 1, part, width), lambda i: (index, 0, i, 0))
    shape = jax.ShapeDtypeStruct((2, 1, rows, width), old.dtype)
    count = len(parts)

    def body(*refs):
        old_ref, first_ref, second_ref = refs[count : count + 3]
        weights_out, first_out, second_out = refs[-3:]
        gradient = refs[0][...].astype(f32)
        for ref in refs[1:count]:
            gradient += ref[...].astype(f32)
        gradient = gradient / loss_scale
        moment_one = beta_one * first_ref[0, 0].astype(f32) + (1.0 - beta_one) * gradient
        moment_two = (
            beta_two * second_ref[0, 0].astype(f32) + (1.0 - beta_two) * gradient * gradient
        )
        updated = old_ref[...].astype(f32) - step_size * moment_one / (
            jnp.sqrt(moment_two) + adam_eps
        )
        weights_out[0, 0] = updated.astype(bf16)
        first_out[0, 0] = moment_one.astype(bf16)
        second_out[0, 0] = moment_two.astype(bf16)

    return pl.pallas_call(
        body,
        grid=(sources,),
        in_specs=[flat] * (count + 1)
        + [moment] * 2
        + [pl.BlockSpec(memory_space=pl.ANY)] * len(results),
        out_specs=[out] * 3,
        out_shape=[shape] * 3,
        input_output_aliases={count + 3 + i: i for i in range(len(results))},
        compiler_params=pltpu.CompilerParams(vmem_limit_bytes=vmem_bytes),
    )(*parts, old, first_old, second_old, *results)


def slot_targets(flat_route, capacity):
    count = flat_route.shape[-1]
    order = jnp.arange(count, dtype=jnp.int32)
    earlier = order[None, :] < order[:, None]
    same = flat_route[:, None] == flat_route[None, :]
    position = jnp.sum((same & earlier).astype(jnp.int32), axis=-1)
    return flat_route * capacity + position


def per_device(
    tokens, routes, router_gates, hidden_cotangent, weights, first_moment, second_moment
):
    row_count, model_width = tokens.shape
    per_token = routes.shape[1]
    hidden_units = hidden_cotangent.shape[2]
    experts = weights.shape[1]
    pieces = model_width // weights.shape[3]
    capacity = 3 * row_count * per_token // (2 * experts)
    routings = row_count * per_token
    half = experts // 2
    mine = lax.axis_index("expert")
    side = mine // half
    local = mine % half
    place = lax.axis_index("dp").astype(jnp.int32).reshape(1)
    swap = [(i, (i + half) % experts) for i in range(experts)]

    def shift(value, step):
        if step % half == 0:
            return value
        pairs = [(i, i // half * half + (i + step) % half) for i in range(experts)]
        return lax.ppermute(value, "expert", pairs)

    def across(value, k):
        return lax.ppermute(value, "dp", [(i, i ^ k) for i in range(pieces)])

    def slot_ids(of_side):
        expert = of_side * half + (local + jnp.arange(half, dtype=jnp.int32)) % half
        return expert[:, None] * capacity + jnp.arange(capacity, dtype=jnp.int32)[None, :]

    def to_owners(part, *earlier):
        by_owner = after(jnp.swapaxes(part, 0, 1), *earlier) if earlier else jnp.swapaxes(part, 0, 1)
        return lax.all_to_all(by_owner, "expert", split_axis=0, concat_axis=0, tiled=True)

    def along_x(part):
        return [across(part, k) for k in range(2, pieces, 2)]

    def both_cores(parts):
        return [piece for one in parts for piece in (one, across(one, 1))]

    def scatter(totals, *earlier):
        terms = [totals[0], across(totals[1], 1)]
        for k in range(2, pieces, 2):
            pair = totals[k].astype(f32) + across(totals[k + 1], 1).astype(f32)
            terms.append(across(after(pair.astype(bf16), *earlier), k))
        return terms

    other_tokens = lax.ppermute(tokens, "expert", swap)
    other_routes = lax.ppermute(routes, "expert", swap)

    gate_factor = router_gates.astype(f32) / gate_unit
    scaled = (gate_factor[:, :, None] * hidden_cotangent.astype(f32)).astype(bf16)
    scaled = scaled.reshape(routings, hidden_units)
    target = slot_targets(routes.reshape(-1), capacity)
    near_ids = slot_ids(side)
    far_ids = slot_ids(1 - side)

    def pick_grads(ids):
        chosen = (target[None, :] == ids.reshape(-1)[:, None]).astype(bf16)
        picked = jnp.dot(chosen, scaled, preferred_element_type=f32).astype(bf16)
        return picked.reshape(half, capacity, hidden_units)

    far_grads = lax.ppermute(pick_grads(far_ids), "expert", swap)

    def pick_matrix(chosen_target):
        by_token = chosen_target.reshape(row_count, per_token)
        hit = by_token[None, :, :] == near_ids.reshape(-1)[:, None, None]
        return jnp.any(hit, axis=2).astype(bf16)

    def send_rows(picker, rows):
        picked = jnp.dot(picker, rows, preferred_element_type=f32).astype(bf16)
        picked = picked.reshape(half, capacity, model_width)
        return [shift(picked[s], s) for s in range(half)]

    near_pick = pick_matrix(target)
    near_rows = send_rows(near_pick, tokens)
    other_tokens = after(other_tokens, other_routes, far_grads, *near_rows[1:])
    other_pick = pick_matrix(slot_targets(other_routes.reshape(-1), capacity))
    far_rows = send_rows(other_pick, other_tokens)
    grads_out = jnp.concatenate([far_grads, pick_grads(near_ids)], axis=1)
    grads_in = [shift(grads_out[s], s) for s in range(half)]

    owned = after(to_owners(weights, other_tokens), *far_rows[1:], *grads_in[1:])
    owned_gate = owned[:, 0].reshape(hidden_units, -1)
    owned_up = owned[:, 1].reshape(hidden_units, -1)
    owned_first = to_owners(first_moment, owned)

    gate_x = along_x(owned_gate)
    up_x = along_x(after(owned_up, *gate_x))
    gate = both_cores([owned_gate] + gate_x)
    up = both_cores([owned_up] + up_x)
    upstream = jnp.swapaxes(jnp.stack(grads_in).reshape(half, 2, capacity, hidden_units), 0, 1)
    upstream = upstream.reshape(2 * half * capacity, hidden_units)

    blocks = far_rows + near_rows
    joined = capacity % 16 != 0
    if joined:
        blocks = [jnp.concatenate(blocks, axis=0)]
    rows, grad_up, factor = forward_gate(place, blocks, upstream, gate)
    up_totals = weight_grads(place, grad_up, rows, pieces)
    up_terms = scatter(up_totals)
    owned_second = to_owners(second_moment, owned_first, up_totals[0])
    grad_gate = forward_up(place, rows, after(factor, owned_first, up_terms[1]), up)
    back = input_grads(
        place, grad_gate, grad_up, gate, up, rows.shape[0] if joined else capacity
    )
    if joined:
        back = [back[0][i * capacity : (i + 1) * capacity] for i in range(2 * half)]
    far_back = [shift(back[s], -s) for s in range(half)]
    near_back = [shift(after(back[half + s], *far_back[1:]), -s) for s in range(half)]
    gate_totals = weight_grads(place, after(grad_gate, *back), rows, pieces)
    gate_terms = scatter(gate_totals)

    def combine(picker, parts):
        parts = jnp.concatenate(parts, axis=0)
        return jnp.einsum("st,sd->td", picker, parts, preferred_element_type=f32)

    far_sum = combine(other_pick, far_back).astype(bf16)
    far_sum = lax.ppermute(far_sum, "expert", swap)
    results = adam(1, up_terms, owned_up, owned_first, owned_second)
    results = adam(0, gate_terms, owned_gate, owned_first, owned_second, *results)
    near_back[1:] = [after(block, *results) for block in near_back[1:]]
    near_sum = combine(near_pick, near_back)
    token_grads = (near_sum + far_sum.astype(f32)).astype(bf16)
    return (token_grads, *results)


def solution(mesh):
    placed = (
        P(("dp", "expert"), None),
        P(("dp", "expert"), None),
        P(("dp", "expert"), None),
        P(("dp", "expert"), None, None),
        P(None, None, "expert", "dp"),
        P(None, None, "expert", "dp"),
        P(None, None, "expert", "dp"),
    )
    return jax.shard_map(
        per_device,
        mesh=mesh,
        in_specs=placed,
        out_specs=(
            P(("dp", "expert"), None),
            P(None, "expert", None, "dp"),
            P(None, "expert", None, "dp"),
            P(None, "expert", None, "dp"),
        ),
        check_vma=False,
    )
```

```python
import jax
import jax.numpy as jnp
from jax import lax
from jax.experimental import pallas as pl
from jax.experimental.pallas import tpu as pltpu
from jax.sharding import PartitionSpec as P

gate_unit = 32768.0
loss_scale = 16.0
beta_one = 0.9
beta_two = 0.95
step_size = 0.001
adam_eps = 1e-08
bf16 = jnp.bfloat16
f32 = jnp.float32
vmem_bytes = 32 * 1024 * 1024


def after(value, *others):
    return lax.optimization_barrier((value, *others))[0]


def tile_of(extent):
    return 256 if extent % 256 == 0 else extent


def whole(shape):
    return pl.BlockSpec(shape, lambda *_: (0,) * len(shape))


def run(body, place, grid, in_specs, out_specs, out_shape, *operands):
    return pl.pallas_call(
        body,
        grid_spec=pltpu.PrefetchScalarGridSpec(
            num_scalar_prefetch=1, grid=grid, in_specs=in_specs, out_specs=out_specs
        ),
        out_shape=out_shape,
        compiler_params=pltpu.CompilerParams(vmem_limit_bytes=vmem_bytes),
    )(place, *operands)


def columns(place, k, width, start=0, size=None):
    first = pl.multiple_of((place[0] ^ k) * width + start, 128)
    return pl.ds(first, width if size is None else size)


def project(place, rows, weights):
    total = None
    for k, piece in enumerate(weights):
        term = lax.dot_general(
            rows[:, columns(place, k, piece.shape[1])],
            piece[...],
            (((1,), (1,)), ((), ())),
            preferred_element_type=f32,
        )
        total = term if total is None else total + term
    return total


def forward_gate(place, blocks, upstream, gate):
    pieces, hidden = len(gate), gate[0].shape[0]
    width = gate[0].shape[1] * pieces
    count = sum(block.shape[0] for block in blocks)
    tile = tile_of(hidden)

    def body(place, *refs):
        block_refs, refs = refs[: len(blocks)], refs[len(blocks) :]
        up_ref, gate_refs = refs[0], refs[1 : 1 + pieces]
        rows, grad_up, factor = refs[1 + pieces :]

        @pl.when(pl.program_id(0) == 0)
        def _():
            first = 0
            for block in block_refs:
                rows[first : first + block.shape[0], :] = block[:, :width]
                first += block.shape[0]

        pre_gate = project(place, rows, gate_refs)
        sigmoid_gate = jax.nn.sigmoid(pre_gate)
        upstream = up_ref[...].astype(f32) * sigmoid_gate
        grad_up[...] = (upstream * pre_gate).astype(bf16)
        factor[...] = upstream * (1.0 + pre_gate * (1.0 - sigmoid_gate))

    part = pl.BlockSpec((count, tile), lambda i, _: (0, i))
    return run(
        body,
        place,
        (hidden // tile,),
        [whole(block.shape) for block in blocks]
        + [part]
        + [pl.BlockSpec((tile, width // pieces), lambda i, _: (i, 0))] * pieces,
        [whole((count, width)), part, part],
        [
            jax.ShapeDtypeStruct((count, width), bf16),
            jax.ShapeDtypeStruct((count, hidden), bf16),
            jax.ShapeDtypeStruct((count, hidden), f32),
        ],
        *blocks,
        upstream,
        *gate,
    )


def forward_up(place, rows, factor, up):
    pieces, hidden = len(up), up[0].shape[0]
    count, width = rows.shape
    tile = tile_of(hidden)

    def body(place, rows, factor, *refs):
        refs[-1][...] = (factor[...] * project(place, rows, refs[:-1])).astype(bf16)

    part = pl.BlockSpec((count, tile), lambda i, _: (0, i))
    return run(
        body,
        place,
        (hidden // tile,),
        [whole((count, width)), part]
        + [pl.BlockSpec((tile, width // pieces), lambda i, _: (i, 0))] * pieces,
        part,
        jax.ShapeDtypeStruct((count, hidden), bf16),
        rows,
        factor,
        *up,
    )


def weight_grads(place, grads, rows, pieces):
    count, hidden = grads.shape
    width = rows.shape[1] // pieces
    tile = tile_of(hidden)

    def body(place, grads, rows, *outs):
        for k, out in enumerate(outs):
            out[...] = lax.dot_general(
                grads[...],
                rows[:, columns(place, k, width)],
                (((0,), (0,)), ((), ())),
                preferred_element_type=f32,
            ).astype(bf16)

    return run(
        body,
        place,
        (hidden // tile,),
        [pl.BlockSpec((count, tile), lambda i, _: (0, i)), whole(rows.shape)],
        [pl.BlockSpec((tile, width), lambda i, _: (i, 0))] * pieces,
        [jax.ShapeDtypeStruct((hidden, width), bf16)] * pieces,
        grads,
        rows,
    )


def input_grads(place, grad_gate, grad_up, gate, up, block_rows):
    count, hidden = grad_gate.shape
    pieces, width = len(gate), gate[0].shape[1]
    tile = tile_of(width)
    blocks = count // block_rows

    def body(place, grad_gate, grad_up, *refs):
        start = pl.program_id(0) * tile
        for k in range(pieces):
            total = jnp.dot(grad_gate[...], refs[k][...], preferred_element_type=f32)
            total += jnp.dot(grad_up[...], refs[pieces + k][...], preferred_element_type=f32)
            total = total.astype(bf16)
            for b, out in enumerate(refs[2 * pieces :]):
                out[:, columns(place, k, width, start, tile)] = total[
                    b * block_rows : (b + 1) * block_rows
                ]

    return run(
        body,
        place,
        (width // tile,),
        [whole((count, hidden))] * 2
        + [pl.BlockSpec((hidden, tile), lambda i, _: (0, i))] * (2 * pieces),
        [whole((block_rows, width * pieces))] * blocks,
        [jax.ShapeDtypeStruct((block_rows, width * pieces), bf16)] * blocks,
        grad_gate,
        grad_up,
        *gate,
        *up,
    )


def adam(index, parts, old, first_old, second_old, *results):
    rows, width = old.shape
    sources, _, part, _ = second_old.shape
    flat = pl.BlockSpec((part, width), lambda i: (i, 0))
    moment = pl.BlockSpec((1, 1, part, width), lambda i: (i, index, 0, 0))
    out = pl.BlockSpec((1, 1, part, width), lambda i: (index, 0, i, 0))
    shape = jax.ShapeDtypeStruct((2, 1, rows, width), old.dtype)
    count = len(parts)

    def body(*refs):
        old_ref, first_ref, second_ref = refs[count : count + 3]
        weights_out, first_out, second_out = refs[-3:]
        gradient = refs[0][...].astype(f32)
        for ref in refs[1:count]:
            gradient += ref[...].astype(f32)
        gradient = gradient / loss_scale
        moment_one = beta_one * first_ref[0, 0].astype(f32) + (1.0 - beta_one) * gradient
        moment_two = (
            beta_two * second_ref[0, 0].astype(f32) + (1.0 - beta_two) * gradient * gradient
        )
        updated = old_ref[...].astype(f32) - step_size * moment_one / (
            jnp.sqrt(moment_two) + adam_eps
        )
        weights_out[0, 0] = updated.astype(bf16)
        first_out[0, 0] = moment_one.astype(bf16)
        second_out[0, 0] = moment_two.astype(bf16)

    return pl.pallas_call(
        body,
        grid=(sources,),
        in_specs=[flat] * (count + 1)
        + [moment] * 2
        + [pl.BlockSpec(memory_space=pl.ANY)] * len(results),
        out_specs=[out] * 3,
        out_shape=[shape] * 3,
        input_output_aliases={count + 3 + i: i for i in range(len(results))},
        compiler_params=pltpu.CompilerParams(vmem_limit_bytes=vmem_bytes),
    )(*parts, old, first_old, second_old, *results)


def slot_targets(flat_route, capacity):
    count = flat_route.shape[-1]
    order = jnp.arange(count, dtype=jnp.int32)
    earlier = order[None, :] < order[:, None]
    same = flat_route[:, None] == flat_route[None, :]
    position = jnp.sum((same & earlier).astype(jnp.int32), axis=-1)
    return flat_route * capacity + position


def per_device(
    tokens, routes, router_gates, hidden_cotangent, weights, first_moment, second_moment
):
    row_count, model_width = tokens.shape
    per_token = routes.shape[1]
    hidden_units = hidden_cotangent.shape[2]
    experts = weights.shape[1]
    pieces = model_width // weights.shape[3]
    capacity = 3 * row_count * per_token // (2 * experts)
    routings = row_count * per_token
    half = experts // 2
    mine = lax.axis_index("expert")
    side = mine // half
    local = mine % half
    place = lax.axis_index("dp").astype(jnp.int32).reshape(1)
    swap = [(i, (i + half) % experts) for i in range(experts)]

    def shift(value, step):
        if step % half == 0:
            return value
        pairs = [(i, i // half * half + (i + step) % half) for i in range(experts)]
        return lax.ppermute(value, "expert", pairs)

    def across(value, k):
        return lax.ppermute(value, "dp", [(i, i ^ k) for i in range(pieces)])

    def slot_ids(of_side):
        expert = of_side * half + (local + jnp.arange(half, dtype=jnp.int32)) % half
        return expert[:, None] * capacity + jnp.arange(capacity, dtype=jnp.int32)[None, :]

    def to_owners(part, *earlier):
        by_owner = after(jnp.swapaxes(part, 0, 1), *earlier) if earlier else jnp.swapaxes(part, 0, 1)
        return lax.all_to_all(by_owner, "expert", split_axis=0, concat_axis=0, tiled=True)

    def along_x(part):
        return [across(part, k) for k in range(2, pieces, 2)]

    def both_cores(parts):
        return [piece for one in parts for piece in (one, across(one, 1))]

    def scatter(totals, *earlier):
        terms = [totals[0], across(totals[1], 1)]
        for k in range(2, pieces, 2):
            pair = totals[k].astype(f32) + across(totals[k + 1], 1).astype(f32)
            terms.append(across(after(pair.astype(bf16), *earlier), k))
        return terms

    other_tokens = lax.ppermute(tokens, "expert", swap)
    other_routes = lax.ppermute(routes, "expert", swap)

    gate_factor = router_gates.astype(f32) / gate_unit
    scaled = (gate_factor[:, :, None] * hidden_cotangent.astype(f32)).astype(bf16)
    scaled = scaled.reshape(routings, hidden_units)
    target = slot_targets(routes.reshape(-1), capacity)
    near_ids = slot_ids(side)
    far_ids = slot_ids(1 - side)

    def pick_grads(ids):
        chosen = (target[None, :] == ids.reshape(-1)[:, None]).astype(bf16)
        picked = jnp.dot(chosen, scaled, preferred_element_type=f32).astype(bf16)
        return picked.reshape(half, capacity, hidden_units)

    far_grads = lax.ppermute(pick_grads(far_ids), "expert", swap)

    def pick_matrix(chosen_target):
        by_token = chosen_target.reshape(row_count, per_token)
        hit = by_token[None, :, :] == near_ids.reshape(-1)[:, None, None]
        return jnp.any(hit, axis=2).astype(bf16)

    def send_rows(picker, rows, grads):
        picked = jnp.dot(picker, rows, preferred_element_type=f32).astype(bf16)
        picked = picked.reshape(half, capacity, model_width)
        picked = jnp.concatenate([picked, grads], axis=2)
        return [shift(picked[s], s) for s in range(half)]

    near_pick = pick_matrix(target)
    near_rows = send_rows(near_pick, tokens, pick_grads(near_ids))
    other_tokens = after(other_tokens, other_routes, far_grads, *near_rows[1:])
    other_pick = pick_matrix(slot_targets(other_routes.reshape(-1), capacity))
    far_rows = send_rows(other_pick, other_tokens, far_grads)
    owned = after(to_owners(weights, other_tokens), *far_rows[1:])
    owned_gate = owned[:, 0].reshape(hidden_units, -1)
    owned_up = owned[:, 1].reshape(hidden_units, -1)
    owned_first = to_owners(first_moment, owned)

    gate_x = along_x(owned_gate)
    up_x = along_x(after(owned_up, *gate_x))
    gate = both_cores([owned_gate] + gate_x)
    up = both_cores([owned_up] + up_x)
    blocks = far_rows + near_rows
    upstream = jnp.concatenate([block[:, model_width:] for block in blocks], axis=0)
    joined = capacity % 16 != 0
    if joined:
        blocks = [jnp.concatenate(blocks, axis=0)]
    rows, grad_up, factor = forward_gate(place, blocks, upstream, gate)
    up_totals = weight_grads(place, grad_up, rows, pieces)
    up_terms = scatter(up_totals)
    owned_second = to_owners(second_moment, owned_first, up_totals[0])
    grad_gate = forward_up(place, rows, after(factor, owned_first), up)
    back = input_grads(
        place, grad_gate, grad_up, gate, up, rows.shape[0] if joined else capacity
    )
    if joined:
        back = [back[0][i * capacity : (i + 1) * capacity] for i in range(2 * half)]
    far_back = [shift(back[s], -s) for s in range(half)]
    near_back = [shift(after(back[half + s], *far_back[1:]), -s) for s in range(half)]
    gate_totals = weight_grads(place, after(grad_gate, *back), rows, pieces)
    gate_terms = scatter(gate_totals, *up_terms)

    def combine(picker, parts):
        parts = jnp.concatenate(parts, axis=0)
        return jnp.einsum("st,sd->td", picker, parts, preferred_element_type=f32)

    far_sum = after(combine(other_pick, far_back).astype(bf16), owned_second, *up_terms)
    far_sum = lax.ppermute(far_sum, "expert", swap)
    results = adam(1, up_terms, owned_up, owned_first, owned_second)
    results = adam(0, gate_terms, owned_gate, owned_first, owned_second, *results)
    near_back[1:] = [after(block, *results) for block in near_back[1:]]
    near_sum = combine(near_pick, near_back)
    token_grads = (near_sum + far_sum.astype(f32)).astype(bf16)
    return (token_grads, *results)


def solution(mesh):
    placed = (
        P(("dp", "expert"), None),
        P(("dp", "expert"), None),
        P(("dp", "expert"), None),
        P(("dp", "expert"), None, None),
        P(None, None, "expert", "dp"),
        P(None, None, "expert", "dp"),
        P(None, None, "expert", "dp"),
    )
    return jax.shard_map(
        per_device,
        mesh=mesh,
        in_specs=placed,
        out_specs=(
            P(("dp", "expert"), None),
            P(None, "expert", None, "dp"),
            P(None, "expert", None, "dp"),
            P(None, "expert", None, "dp"),
        ),
        check_vma=False,
    )
```
